32 devices in a mesh: pairs: 8 (over z, x), rep: 4 (over y, core).
Axes of the slice: x: 2, y: 2, z: 4, core: 2. Of those that a mesh axis runs over, the one named last changes fastest.
Arguments:
- factors: bfloat16 [8, 512, 512], P('pairs', 'rep'), may hold values from -1.1953125 to 1.1953125
- orbital_virtuals: bfloat16 [8, 512, 128], P('pairs'), may hold values from -0.25 to 0.25
- occupied: bfloat16 [8], P('pairs'), may hold values from -1.5 to -0.29882812
- pair_rotations: bfloat16 [256, 2, 128, 128], P('pairs'), may hold values from -0.5 to 0.5
- pair_energies: float32 [256, 2, 128], P('pairs'), may hold values from 0.5 to 4
- pair_orbitals: int32 [256, 2], P('pairs'), may hold values from 0 to 7
- pair_ranks: int32 [256], P('pairs'), may hold values from 32 to 128
- margins: bfloat16 [256, 6, 128, 128], P('pairs'), may hold values from -0.5 to 0.5
- coupling_weight: float32 [256, 6], P('pairs'), may hold values from -4 to 4
- send_slots: int32 [8, 8, 2], P('pairs'), may hold values from 0 to 31
- couplings: int32 [256, 6], P('pairs'), may hold values from 0 to 15
Outputs:
- amplitudes: bfloat16 [256, 128, 128], P('pairs')
- densities: float32 [8, 128, 128], P('pairs')
The draws below stay inside these ranges and needn't reach their ends.
Inputs may be any that keep to these rules, and one draw needn't show every extreme that they name: `pair_orbitals`: the first and second orbital of a pair; they may be equal. `pair_ranks`: positions at or past a pair's rank are padding. send_slots[q, d, s] is the local pair, on index q of pairs, whose amplitudes fill slot s of what q sends to index d. `couplings`: entry k of a pair on index d names slot k % 2 of what index k // 2 sends to d.
All inputs are finite; a program needn't handle non-finite values.
Results may differ from the reference program's by a relative error of at most 0.0085.
Values may be sent and summed in bfloat16 or wider, within the bound.
A program may use at most 64 MiB of HBM per device.

```python
import math
import jax
import jax.numpy as jnp
from jax import lax

NAUX = 512
NPAO = 512
RANK = 128
PAIR_DEV = 32
NCOUP = 6
CAPA = 2
ITERS = 3
OWNERS = 8
NORB = 8
NPAIR = 256


def plant(drawn, key, least, top_value):
    index_at = [jax.random.randint(jax.random.fold_in(key, axis), (), 0, length) for axis, length in enumerate(drawn.shape)]
    widest = drawn.shape.index(max(drawn.shape))
    next_to = index_at[:widest] + [(index_at[widest] + 1) % drawn.shape[widest]] + index_at[widest + 1:]
    return drawn.at[tuple(index_at)].set(least).at[tuple(next_to)].set(top_value)


def levels(key, extent, cuts, low, largest):
    loudness, own = 1.0, jax.random.fold_in(key, 6)
    for position, parts in cuts:
        heights = jnp.exp(jax.random.uniform(jax.random.fold_in(own, position), (parts,), jnp.float32, low / len(cuts), largest / len(cuts)))
        loudness = loudness * jnp.repeat(heights, extent[position] // parts).reshape([-1 if axis == position else 1 for axis in range(len(extent))])
    return loudness


def gaussian(rng, shape, spread, bound, pieces=(), held_as=jnp.bfloat16):
    gain = levels(rng, shape, pieces, -0.22, 0.18) if pieces else 1.0
    drawn = jax.random.normal(rng, shape, jnp.float32) * spread * gain
    return jnp.minimum(jnp.maximum(drawn, -bound), bound).astype(held_as)


def setup_inputs(seed: int = 0) -> dict:
    splits = jax.random.split(jax.random.key(seed), 12)
    factors = gaussian(splits[0], (NORB, NAUX, NPAO), 0.2, 1.1953125, ((0, 8), (1, 4)))
    orbital_virtuals = gaussian(splits[1], (NORB, NPAO, RANK), NPAO ** -0.5, 0.25, ((0, 8),))
    occupied = jnp.clip(-1.5 + 1.2011719 * jax.random.uniform(splits[2], (NORB,), jnp.float32) ** levels(splits[2], (NORB,), ((0, 8),), -0.2, 0.2), -1.5, -0.29882812).astype(jnp.bfloat16)
    pair_rotations = gaussian(splits[3], (NPAIR, 2, RANK, RANK), RANK ** -0.5, 0.5, ((0, 8),))
    pair_energies = jnp.clip(jnp.exp(math.log(4.0) - 2.0794415 * jax.random.uniform(splits[4], (NPAIR, 2, RANK), jnp.float32) ** levels(splits[4], (NPAIR, 2, RANK), ((0, 8),), -0.2, 0.2)), 0.5, 4.0)
    pair_orbitals = plant(jax.random.randint(splits[5], (NPAIR, 2), 0, NORB), jax.random.fold_in(splits[5], 1), 0, NORB - 1).astype(jnp.int32)
    pair_ranks = plant(jax.random.randint(splits[6], (NPAIR,), RANK // 4, RANK + 1), jax.random.fold_in(splits[6], 1), RANK // 4, RANK).astype(jnp.int32)
    margins = gaussian(splits[7], (NPAIR, NCOUP, RANK, RANK), RANK ** -0.5, 0.5, ((0, 8),))
    coupling_weight = jnp.clip(jax.random.uniform(splits[8], (NPAIR, NCOUP), jnp.float32, -4.0, 4.0) * levels(splits[8], (NPAIR, NCOUP), ((0, 8),), -0.4, 0.0), -4.0, 4.0)
    send_slots = plant(jax.random.randint(splits[9], (OWNERS, OWNERS, CAPA), 0, PAIR_DEV), jax.random.fold_in(splits[9], 1), 0, PAIR_DEV - 1).astype(jnp.int32)
    couplings = plant(jax.random.randint(splits[10], (NPAIR, NCOUP), 0, OWNERS * CAPA), jax.random.fold_in(splits[10], 1), 0, (OWNERS * CAPA) - 1).astype(jnp.int32)
    return dict(factors=factors, orbital_virtuals=orbital_virtuals, occupied=occupied, pair_rotations=pair_rotations, pair_energies=pair_energies, pair_orbitals=pair_orbitals, pair_ranks=pair_ranks, margins=margins, coupling_weight=coupling_weight, send_slots=send_slots, couplings=couplings)


def reference(factors, orbital_virtuals, occupied, pair_rotations, pair_energies, pair_orbitals, pair_ranks, margins, coupling_weight, send_slots, couplings):
    halves = jnp.einsum("oxp,opr->oxr", factors.astype(jnp.float32), orbital_virtuals.astype(jnp.float32), precision=lax.Precision.HIGHEST).astype(jnp.bfloat16)
    rank_size = pair_rotations.shape[-1]
    positions = jnp.arange(rank_size, dtype=jnp.int32)
    visible = (positions[None, :] < pair_ranks[:, None]).astype(jnp.float32)
    mask_pair = visible[:, :, None] * visible[:, None, :]
    occ_pair = occupied[pair_orbitals[:, 0]].astype(jnp.float32) + occupied[pair_orbitals[:, 1]].astype(jnp.float32)
    denominator = pair_energies[:, 0, :, None] + pair_energies[:, 1, None, :] - occ_pair[:, None, None]

    def integral_block(block_index):
        first_row = (block_index * PAIR_DEV).astype(jnp.int32)
        orbital_rows = lax.dynamic_slice_in_dim(pair_orbitals, first_row, PAIR_DEV, 0)
        rotations = lax.dynamic_slice_in_dim(pair_rotations, first_row, PAIR_DEV, 0).astype(jnp.float32)
        left_half = halves[orbital_rows[:, 0]].astype(jnp.float32)
        right_half = halves[orbital_rows[:, 1]].astype(jnp.float32)
        mixed_pair = jnp.einsum("pxa,pxb->pab", left_half, right_half, precision=lax.Precision.HIGHEST)
        half_turn = jnp.einsum("pxa,pxy->pay", rotations[:, 0], mixed_pair, precision=lax.Precision.HIGHEST)
        return jnp.einsum("pay,pyb->pab", half_turn, rotations[:, 1], precision=lax.Precision.HIGHEST)

    block_ids = jnp.arange(OWNERS, dtype=jnp.int32)
    integral = lax.map(integral_block, block_ids).reshape(NPAIR, rank_size, rank_size) * mask_pair
    device_index = jnp.arange(NPAIR, dtype=jnp.int32) // PAIR_DEV
    source = couplings // CAPA
    slot_index = couplings % CAPA
    partner = source * PAIR_DEV + send_slots[source, device_index[:, None], slot_index]
    amplitude = (-integral / denominator).astype(jnp.bfloat16)
    for iteration in range(ITERS):
        def relax_block(block_index, current=amplitude):
            first_row = (block_index * PAIR_DEV).astype(jnp.int32)
            links = lax.dynamic_slice_in_dim(partner, first_row, PAIR_DEV, 0)
            partner_amp = current[links].astype(jnp.float32)
            margin_rows = lax.dynamic_slice_in_dim(margins, first_row, PAIR_DEV, 0).astype(jnp.float32)
            left_turn = jnp.einsum("pcab,pcbd->pcad", margin_rows, partner_amp, precision=lax.Precision.HIGHEST).astype(jnp.bfloat16)
            left_turn = lax.optimization_barrier(left_turn).astype(jnp.float32)
            transformed = jnp.einsum("pcad,pced->pcae", left_turn, margin_rows, precision=lax.Precision.HIGHEST)
            weight = lax.dynamic_slice_in_dim(coupling_weight, first_row, PAIR_DEV, 0)
            coupled = jnp.einsum("pc,pcae->pae", weight, transformed, precision=lax.Precision.HIGHEST)
            integral_rows = lax.dynamic_slice_in_dim(integral, first_row, PAIR_DEV, 0)
            denominator_rows = lax.dynamic_slice_in_dim(denominator, first_row, PAIR_DEV, 0)
            mask_rows = lax.dynamic_slice_in_dim(mask_pair, first_row, PAIR_DEV, 0)
            return (-(integral_rows - coupled) / denominator_rows * mask_rows).astype(jnp.bfloat16)

        amplitude = lax.map(relax_block, block_ids).reshape(NPAIR, rank_size, rank_size)
    rotations = pair_rotations.astype(jnp.float32)
    amplitude_wide = amplitude.astype(jnp.float32)
    side_left = jnp.einsum("pxa,pab->pxb", rotations[:, 0], amplitude_wide, precision=lax.Precision.HIGHEST).astype(jnp.bfloat16)
    side_right = jnp.einsum("pyb,pab->pya", rotations[:, 1], amplitude_wide, precision=lax.Precision.HIGHEST).astype(jnp.bfloat16)
    side_left = lax.optimization_barrier(side_left).astype(jnp.float32)
    side_right = lax.optimization_barrier(side_right).astype(jnp.float32)
    gram_left = jnp.einsum("pxb,pzb->pxz", side_left, side_left, precision=lax.Precision.HIGHEST)
    gram_right = jnp.einsum("pxb,pzb->pxz", side_right, side_right, precision=lax.Precision.HIGHEST)
    densities = jax.ops.segment_sum(gram_left, pair_orbitals[:, 0], NORB) + jax.ops.segment_sum(gram_right, pair_orbitals[:, 1], NORB)
    return amplitude, densities / rank_size
```

```python
import functools

import jax
import jax.numpy as jnp
from jax import lax
from jax.experimental import pallas as pl
from jax.experimental.pallas import tpu as pltpu
from jax.sharding import PartitionSpec as P

ITERS = 3
OCC_ROWS = 16
CHUNKS = 4
F32 = jnp.float32
BF16 = jnp.bfloat16


def dot_nn(a, b):
    return lax.dot_general(a, b, (((1,), (0,)), ((), ())), preferred_element_type=F32)


def dot_nt(a, b):
    return lax.dot_general(a, b, (((1,), (1,)), ((), ())), preferred_element_type=F32)


def two_parts(x):
    high = x.astype(BF16)
    low = (x - high.astype(F32)).astype(BF16)
    return jnp.concatenate([high, low], axis=0)


def kernel(
    groups,
    reps,
    factors_ref,
    virtuals_ref,
    occ_ref,
    energy_ref,
    orbitals_ref,
    ranks_ref,
    weight_ref,
    slots_ref,
    couplings_ref,
    rotations_hbm,
    margins_hbm,
    amp_ref,
    dens_ref,
    rot,
    margin,
    turn,
    halves,
    sbuf,
    slots,
    local,
    integ,
    scale,
    afin,
    grams,
    dsend1,
    drecv1,
    dsend2,
    drecv2,
    dfin,
    load_sem,
    s1,
    r1,
    ys,
    yr,
    ss,
    sr,
    fs,
    fr,
    d1s,
    d1r,
    d2s,
    d2r,
    d3s,
    d3r,
):
    me = lax.axis_index("pairs")
    rep = lax.axis_index("rep")
    sides = 2 if reps % 2 == 0 else 1
    lanes = reps // sides
    side = lax.rem(rep, sides)
    lane = rep // sides
    orbs, aux = factors_ref.shape[:2]
    pairs, _, rank, _ = rot.shape
    coups = margin.shape[1]
    rows = rank // reps
    capa = slots_ref.shape[1]
    norb = groups * orbs
    part = pairs // CHUNKS
    row0 = pl.multiple_of(rep * rows, rows)

    def lane_rep(step):
        return lax.rem(lane + step + lanes, lanes) * sides + side

    twin = lane * sides + (1 - side)

    def send(src, dst, ssem, rsem, group, to_rep):
        return pltpu.make_async_remote_copy(
            src_ref=src,
            dst_ref=dst,
            send_sem=ssem,
            recv_sem=rsem,
            device_id=(group, to_rep),
            device_id_type=pl.DeviceIdType.MESH,
        )

    rot_copy = pltpu.make_async_copy(rotations_hbm, rot, load_sem.at[0])
    rot_copy.start()
    margin_copy = pltpu.make_async_copy(margins_hbm, margin, load_sem.at[1])
    margin_copy.start()

    barrier = pltpu.get_barrier_semaphore()

    def greet(k, carry):
        pl.semaphore_signal(
            barrier,
            inc=1,
            device_id=(lax.rem(me + k, groups), rep),
            device_id_type=pl.DeviceIdType.MESH,
        )
        return carry

    lax.fori_loop(1, groups, greet, 0)
    for j in range(1, reps):
        pl.semaphore_signal(
            barrier,
            inc=1,
            device_id=(me, lax.rem(rep + j, reps)),
            device_id_type=pl.DeviceIdType.MESH,
        )

    for o in range(orbs):
        half = dot_nn(factors_ref[o], virtuals_ref[o]).astype(BF16)
        halves[rep, me * orbs + o, :aux, :] = half
        halves[rep, me * orbs + o, aux:, :] = occ_ref[o]

    rot_copy.wait()

    def flip(p, carry):
        turn[p] = rot[p, 0].astype(F32).T.astype(BF16)
        return carry

    lax.fori_loop(0, pairs, flip, 0, unroll=4)
    pl.semaphore_wait(barrier, groups - 1 + reps - 1)

    def group_copy(e, k, src, here):
        to = lax.rem(me + k, groups)
        return send(src(to), here(rep, me), s1.at[e, k], r1.at[e, k], to, rep)

    def lane_copy(e, j, k, here, q):
        block = here(rep, q)
        return send(block, block, ys.at[e, j, k], yr.at[e, j, k], me, lane_rep(j))

    def twin_copy(e, j, k, here, q):
        block = here(lane_rep(-j), q)
        return send(block, block, ss.at[e, j, k], sr.at[e, j, k], me, twin)

    def spread(e, src, here):
        def forward(k, carry):
            q = lax.rem(me - k + groups, groups)
            for j in range(1, lanes):
                lane_copy(e, j, k, here, q).start()
            if sides == 2:
                twin_copy(e, 0, k, here, q).start()
            return carry

        def arrive(k, carry):
            q = lax.rem(me - k + groups, groups)
            send(src(me), here(rep, q), s1.at[e, k], r1.at[e, k], me, rep).wait_recv()
            return forward(k, carry)

        def relay(k, carry):
            q = lax.rem(me - k + groups, groups)
            for j in range(1, lanes):
                block = here(lane_rep(-j), q)
                send(block, block, ys.at[e, j, k], yr.at[e, j, k], me, rep).wait_recv()
                if sides == 2:
                    twin_copy(e, j, k, here, q).start()
            return carry

        def settle(k, carry):
            q = lax.rem(me - k + groups, groups)
            for j in range(lanes):
                if sides == 2:
                    other = lax.rem(lane - j + lanes, lanes) * sides + (1 - side)
                    block = here(other, q)
                    send(block, block, ss.at[e, j, k], sr.at[e, j, k], me, rep).wait_recv()
            return carry

        def sent(k, carry):
            q = lax.rem(me - k + groups, groups)
            for j in range(1, lanes):
                lane_copy(e, j, k, here, q).wait_send()
            if sides == 2:
                for j in range(lanes):
                    twin_copy(e, j, k, here, q).wait_send()
            return carry

        def sent_group(k, carry):
            group_copy(e, k, src, here).wait_send()
            return carry

        forward(0, 0)
        lax.fori_loop(1, groups, arrive, 0)
        lax.fori_loop(0, groups, relay, 0)
        lax.fori_loop(0, groups, settle, 0)
        lax.fori_loop(0, groups, sent, 0)
        lax.fori_loop(1, groups, sent_group, 0)

    def half_place(r, q):
        return halves.at[r, pl.ds(q * orbs, orbs)]

    def half_source(d):
        return halves.at[rep, pl.ds(me * orbs, orbs)]

    def start_half(k, carry):
        group_copy(0, k, half_source, half_place).start()
        return carry

    lax.fori_loop(1, groups, start_half, 0)
    spread(0, half_source, half_place)

    row_at = lax.broadcasted_iota(jnp.int32, (rows, rank), 0) + row0
    column_at = lax.broadcasted_iota(jnp.int32, (rows, rank), 1)

    def integrate(p, carry):
        i = orbitals_ref[p, 0]
        j = orbitals_ref[p, 1]
        left = halves[:, i]
        right = halves[:, j]
        left_half = left[:, :aux].reshape(reps * aux, rank)
        right_half = right[:, :aux].reshape(reps * aux, rank)
        turned = two_parts(dot_nt(turn[p, pl.ds(row0, rows), :], left_half))
        mixed = dot_nn(turned, right_half)
        mixed = two_parts(mixed[:rows] + mixed[rows:])
        value = dot_nn(mixed, rot[p, 1])
        value = value[:rows] + value[rows:]
        occ = left[0, aux:].astype(F32)[:1] + right[0, aux:].astype(F32)[:1]
        live = (row_at < ranks_ref[0, p]) & (column_at < ranks_ref[0, p])
        factor = jnp.where(live, -1.0 / (energy_ref[p] - occ), 0.0)
        integ[p] = value
        scale[p] = factor
        local[p] = (value * factor).astype(BF16)
        return carry

    lax.fori_loop(0, pairs, integrate, 0, unroll=2)
    margin_copy.wait()

    def iterate(it, done):
        e = (it + 1) % 2

        def slot_place(r, q):
            return slots[it].at[r, pl.ds(q * capa, capa)]

        def slot_source(d):
            return sbuf.at[it, d]

        def post(k, carry):
            to = lax.rem(me + k, groups)
            for s in range(capa):
                sbuf[it, to, s] = local[slots_ref[to, s]]
            group_copy(e, k, slot_source, slot_place).start()
            return carry

        for s in range(capa):
            slots[it][rep, me * capa + s] = local[slots_ref[me, s]]
        lax.fori_loop(1, groups, post, 0)
        spread(e, slot_source, slot_place)

        def relax(p, carry):
            coupled = jnp.zeros((rows, rank), F32)
            for c in range(coups):
                amp = slots[it][:, couplings_ref[p, c]].reshape(rank, rank)
                left = dot_nn(margin[p, c, pl.ds(row0, rows), :], amp).astype(BF16)
                coupled = coupled + weight_ref[p, c] * dot_nt(left, margin[p, c])
            moved = ((integ[p] - coupled) * scale[p]).astype(BF16)
            if it == ITERS - 1:
                afin[rep, p] = moved
            else:
                local[p] = moved
            return carry

        for chunk in range(CHUNKS):
            lax.fori_loop(chunk * part, (chunk + 1) * part, relax, 0, unroll=2)
            done(chunk)

    for it in range(ITERS - 1):
        iterate(it, lambda chunk: None)

    def piece(r, chunk):
        return afin.at[r, pl.ds(chunk * part, part)]

    def final_lane(j, chunk):
        block = piece(rep, chunk)
        return send(block, block, fs.at[j, chunk], fr.at[j, chunk], me, lane_rep(j))

    def final_twin(j, chunk):
        block = piece(lane_rep(-j), chunk)
        index = lanes + j
        return send(block, block, fs.at[index, chunk], fr.at[index, chunk], me, twin)

    def publish(chunk):
        for j in range(1, lanes):
            final_lane(j, chunk).start()
        if sides == 2:
            final_twin(0, chunk).start()

    iterate(ITERS - 1, publish)

    for chunk in range(CHUNKS):
        for j in range(1, lanes):
            block = piece(lane_rep(-j), chunk)
            send(block, block, fs.at[j, chunk], fr.at[j, chunk], me, rep).wait_recv()
            if sides == 2:
                final_twin(j, chunk).start()
    for chunk in range(CHUNKS):
        if sides == 2:
            for j in range(lanes):
                other = lax.rem(lane - j + lanes, lanes) * sides + (1 - side)
                block = piece(other, chunk)
                index = lanes + j
                send(block, block, fs.at[index, chunk], fr.at[index, chunk], me, rep).wait_recv()

    def lay(p, carry):
        for r in range(reps):
            amp_ref[p, r * rows : (r + 1) * rows, :] = afin[r, p]
        return carry

    lax.fori_loop(0, pairs, lay, 0, unroll=4)

    share = pairs // reps
    base = rep * share

    def gram(k, carry):
        amp = afin[:, base + k].reshape(rank, rank)
        side_left = dot_nn(rot[base + k, 0], amp).astype(BF16)
        side_right = dot_nt(rot[base + k, 1], amp).astype(BF16)
        grams[2 * k] = dot_nt(side_left, side_left) * (1.0 / rank)
        grams[2 * k + 1] = dot_nt(side_right, side_right) * (1.0 / rank)
        return carry

    lax.fori_loop(0, share, gram, 0, unroll=2)

    def collect(o, carry):
        for r in range(reps):
            span = slice(r * rows, (r + 1) * rows)
            total = jnp.zeros((rows, rank), F32)
            for k in range(share):
                for s in range(2):
                    named = orbitals_ref[base + k, s] == o
                    total = total + jnp.where(named, grams[2 * k + s, span, :], 0.0)
            dsend1[r, o] = total.astype(BF16)
        return carry

    lax.fori_loop(0, norb, collect, 0)

    def density_rep(j):
        to = lax.rem(rep + j, reps)
        return send(dsend1.at[to], drecv1.at[rep], d1s.at[j], d1r.at[j], me, to)

    for j in range(1, reps):
        density_rep(j).start()
    drecv1[rep] = dsend1[rep]
    for j in range(1, reps):
        block = drecv1.at[lax.rem(rep - j + reps, reps)]
        send(block, block, d1s.at[j], d1r.at[j], me, rep).wait_recv()

    def density_group(k):
        to = lax.rem(me + k, groups)
        return send(dsend2.at[to], drecv2.at[me], d2s.at[k], d2r.at[k], to, rep)

    def rep_sum(d):
        total = jnp.zeros((orbs, rows, rank), F32)
        for r in range(reps):
            total = total + drecv1[r, pl.ds(d * orbs, orbs)].astype(F32)
        return total

    def post_density(k, carry):
        to = lax.rem(me + k, groups)
        dsend2[to] = rep_sum(to).astype(BF16)
        density_group(k).start()
        return carry

    lax.fori_loop(1, groups, post_density, 0)
    own = rep_sum(me)

    def take_density(k, total):
        q = lax.rem(me - k + groups, groups)
        block = drecv2.at[q]
        send(block, block, d2s.at[k], d2r.at[k], me, rep).wait_recv()
        return total + drecv2[q].astype(F32)

    dfin[rep] = lax.fori_loop(1, groups, take_density, own)

    def density_last(j):
        to = lax.rem(rep + j, reps)
        return send(dfin.at[rep], dfin.at[rep], d3s.at[j], d3r.at[j], me, to)

    for j in range(1, reps):
        density_last(j).start()
    for j in range(1, reps):
        block = dfin.at[lax.rem(rep - j + reps, reps)]
        send(block, block, d3s.at[j], d3r.at[j], me, rep).wait_recv()
    for r in range(reps):
        dens_ref[:, r * rows : (r + 1) * rows, :] = dfin[r]

    for chunk in range(CHUNKS):
        for j in range(1, lanes):
            final_lane(j, chunk).wait_send()
        if sides == 2:
            for j in range(lanes):
                final_twin(j, chunk).wait_send()
    for j in range(1, reps):
        density_rep(j).wait_send()
        density_last(j).wait_send()

    def sent_density(k, carry):
        density_group(k).wait_send()
        return carry

    lax.fori_loop(1, groups, sent_density, 0)


def body(
    factors,
    orbital_virtuals,
    occupied,
    pair_rotations,
    pair_energies,
    pair_orbitals,
    pair_ranks,
    margins,
    coupling_weight,
    send_slots,
    couplings,
):
    groups = lax.axis_size("pairs")
    reps = lax.axis_size("rep")
    orbs, aux, _ = factors.shape
    pairs, _, rank, _ = pair_rotations.shape
    coups = margins.shape[1]
    capa = send_slots.shape[2]
    rows = rank // reps
    norb = groups * orbs
    share = pairs // reps
    sides = 2 if reps % 2 == 0 else 1
    lanes = reps // sides
    own_rows = lax.dynamic_slice_in_dim(
        pair_energies[:, 0], lax.axis_index("rep") * rows, rows, 1
    )
    energy = own_rows[:, :, None] + pair_energies[:, 1][:, None, :]
    occ = jnp.broadcast_to(occupied[:, None, None], (orbs, OCC_ROWS, rank))
    vmem = pl.BlockSpec(memory_space=pltpu.VMEM)
    smem = pl.BlockSpec(memory_space=pltpu.SMEM)
    anywhere = pl.BlockSpec(memory_space=pl.ANY)
    dma = pltpu.SemaphoreType.DMA
    return pl.pallas_call(
        functools.partial(kernel, groups, reps),
        out_shape=(
            jax.ShapeDtypeStruct((pairs, rank, rank), BF16),
            jax.ShapeDtypeStruct((orbs, rank, rank), F32),
        ),
        in_specs=[vmem] * 4 + [smem] * 5 + [anywhere] * 2,
        out_specs=(vmem, vmem),
        scratch_shapes=[
            pltpu.VMEM(pair_rotations.shape, BF16),
            pltpu.VMEM(margins.shape, BF16),
            pltpu.VMEM((pairs, rank, rank), BF16),
            pltpu.VMEM((reps, norb, aux + OCC_ROWS, rank), BF16),
            pltpu.VMEM((ITERS, groups, capa, rows, rank), BF16),
            tuple(
                pltpu.VMEM((reps, groups * capa, rows, rank), BF16) for _ in range(ITERS)
            ),
            pltpu.VMEM((pairs, rows, rank), BF16),
            pltpu.VMEM((pairs, rows, rank), F32),
            pltpu.VMEM((pairs, rows, rank), F32),
            pltpu.VMEM((reps, pairs, rows, rank), BF16),
            pltpu.VMEM((2 * share, rank, rank), F32),
            pltpu.VMEM((reps, norb, rows, rank), BF16),
            pltpu.VMEM((reps, norb, rows, rank), BF16),
            pltpu.VMEM((groups, orbs, rows, rank), BF16),
            pltpu.VMEM((groups, orbs, rows, rank), BF16),
            pltpu.VMEM((reps, orbs, rows, rank), F32),
            dma((2,)),
            dma((2, groups)),
            dma((2, groups)),
            dma((2, lanes, groups)),
            dma((2, lanes, groups)),
            dma((2, lanes, groups)),
            dma((2, lanes, groups)),
            dma((2 * lanes, CHUNKS)),
            dma((2 * lanes, CHUNKS)),
            dma((reps,)),
            dma((reps,)),
            dma((groups,)),
            dma((groups,)),
            dma((reps,)),
            dma((reps,)),
        ],
        compiler_params=pltpu.CompilerParams(
            collective_id=0, has_side_effects=True, vmem_limit_bytes=60 * 1024 * 1024
        ),
        cost_estimate=pl.CostEstimate(
            flops=4 * pairs * coups * ITERS * rows * rank * rank,
            bytes_accessed=2 * pairs * coups * rank * rank,
            transcendentals=0,
        ),
    )(
        factors,
        orbital_virtuals,
        occ,
        energy,
        pair_orbitals,
        pair_ranks[None, :],
        coupling_weight,
        send_slots[0],
        couplings,
        pair_rotations,
        margins,
    )


def solution(mesh):
    return jax.shard_map(
        body,
        mesh=mesh,
        in_specs=(
            P("pairs", "rep", None),
            P("pairs", None, None),
            P("pairs"),
            P("pairs", None, None, None),
            P("pairs", None, None),
            P("pairs", None),
            P("pairs"),
            P("pairs", None, None, None),
            P("pairs", None),
            P("pairs", None, None),
            P("pairs", None),
        ),
        out_specs=(P("pairs", None, None), P("pairs", None, None)),
        check_vma=False,
    )
```

```python
import functools

import jax
import jax.numpy as jnp
from jax import lax
from jax.experimental import pallas as pl
from jax.experimental.pallas import tpu as pltpu
from jax.sharding import PartitionSpec as P

ITERS = 3
OCC_ROWS = 16
UNROLL = 8
F32 = jnp.float32
BF16 = jnp.bfloat16


def dot_nn(a, b):
    return lax.dot_general(a, b, (((1,), (0,)), ((), ())), preferred_element_type=F32)


def dot_nt(a, b):
    return lax.dot_general(a, b, (((1,), (1,)), ((), ())), preferred_element_type=F32)


def two_parts(x):
    high = x.astype(BF16)
    low = (x - high.astype(F32)).astype(BF16)
    return jnp.concatenate([high, low], axis=0)


def kernel(
    groups,
    reps,
    factors_ref,
    virtuals_ref,
    occ_ref,
    energies_ref,
    orbitals_ref,
    ranks_ref,
    weight_ref,
    slots_ref,
    couplings_ref,
    rotations_hbm,
    margins_hbm,
    amp_ref,
    dens_ref,
    rot,
    margin,
    turn,
    halves,
    sbuf,
    slots,
    local,
    integ,
    scale,
    afin,
    grams,
    dsend1,
    drecv1,
    dsend2,
    drecv2,
    dfin,
    load_sem,
    s1,
    r1,
    ys,
    yr,
    ss,
    sr,
    fs,
    fr,
    d1s,
    d1r,
    d2s,
    d2r,
    d3s,
    d3r,
):
    me = lax.axis_index("pairs")
    rep = lax.axis_index("rep")
    sides = 2 if reps % 2 == 0 else 1
    lanes = reps // sides
    side = lax.rem(rep, sides)
    lane = rep // sides
    orbs, aux = factors_ref.shape[:2]
    pairs, _, rank, _ = rot.shape
    coups = margin.shape[1]
    rows = rank // reps
    capa = slots_ref.shape[0]
    norb = groups * orbs
    share = pairs // reps
    row0 = pl.multiple_of(rep * rows, rows)

    def lane_rep(step):
        return lax.rem(lane + step + lanes, lanes) * sides + side

    twin = lane * sides + (1 - side)

    def send(src, dst, ssem, rsem, group, to_rep):
        return pltpu.make_async_remote_copy(
            src_ref=src,
            dst_ref=dst,
            send_sem=ssem,
            recv_sem=rsem,
            device_id=(group, to_rep),
            device_id_type=pl.DeviceIdType.MESH,
        )

    rot_copy = pltpu.make_async_copy(rotations_hbm, rot, load_sem.at[0])
    rot_copy.start()
    margin_copy = pltpu.make_async_copy(margins_hbm, margin, load_sem.at[1])
    margin_copy.start()

    barrier = pltpu.get_barrier_semaphore()

    def greet(k, carry):
        pl.semaphore_signal(
            barrier,
            inc=1,
            device_id=(lax.rem(me + k, groups), rep),
            device_id_type=pl.DeviceIdType.MESH,
        )
        return carry

    lax.fori_loop(1, groups, greet, 0)
    for j in range(1, reps):
        pl.semaphore_signal(
            barrier,
            inc=1,
            device_id=(me, lax.rem(rep + j, reps)),
            device_id_type=pl.DeviceIdType.MESH,
        )

    for o in range(orbs):
        half = dot_nn(factors_ref[o], virtuals_ref[o]).astype(BF16)
        level = jnp.broadcast_to(occ_ref[o : o + 1].astype(F32), (OCC_ROWS, rank))
        halves[0][me * orbs + o, :aux, :] = half
        halves[0][me * orbs + o, aux:, :] = level.astype(BF16)

    pl.semaphore_wait(barrier, groups - 1 + reps - 1)

    def group_copy(e, k, src, here):
        to = lax.rem(me + k, groups)
        return send(src(to), here(0, 0, me), s1.at[e, k], r1.at[e, k], to, rep)

    def spread(e, src, here, land, between, ready):
        def source(k):
            return lax.rem(me - k + groups, groups)

        def lane_copy(j, k):
            q = source(k)
            return send(
                here(0, 0, q), land(j, 0, q), ys.at[e, j, k], yr.at[e, j, k], me, lane_rep(j)
            )

        def twin_copy(j, k):
            q = source(k)
            return send(here(j, 0, q), land(j, 1, q), ss.at[e, j, k], sr.at[e, j, k], me, twin)

        def took(place, ssem, rsem):
            send(place, place, ssem, rsem, me, twin).wait_recv()

        def forward(k, carry):
            for j in range(1, lanes):
                lane_copy(j, k).start()
            if sides == 2:
                twin_copy(0, k).start()
            return carry

        def arrive(k, carry):
            between(k)
            took(here(0, 0, source(k)), s1.at[e, k], r1.at[e, k])
            return forward(k, carry)

        forward(0, 0)
        lax.fori_loop(1, groups, arrive, 0)
        ready(0, 0)

        for j in range(1, lanes):

            def relay(k, carry, j=j):
                took(here(j, 0, source(k)), ys.at[e, j, k], yr.at[e, j, k])
                if sides == 2:
                    twin_copy(j, k).start()
                return carry

            lax.fori_loop(0, groups, relay, 0)
            ready(j, 0)

        if sides == 2:
            for j in range(lanes):

                def settle(k, carry, j=j):
                    took(here(j, 1, source(k)), ss.at[e, j, k], sr.at[e, j, k])
                    return carry

                lax.fori_loop(0, groups, settle, 0)
                ready(j, 1)

        def sent(k, carry):
            for j in range(1, lanes):
                lane_copy(j, k).wait_send()
            if sides == 2:
                for j in range(lanes):
                    twin_copy(j, k).wait_send()
            return carry

        def sent_group(k, carry):
            group_copy(e, k, src, here).wait_send()
            return carry

        def finish():
            lax.fori_loop(0, groups, sent, 0)
            lax.fori_loop(1, groups, sent_group, 0)

        return finish

    def half_place(j, t, q):
        return halves[j * sides + t].at[pl.ds(q * orbs, orbs)]

    def half_source(d):
        return half_place(0, 0, me)

    def start_half(k, carry):
        group_copy(0, k, half_source, half_place).start()
        return carry

    lax.fori_loop(1, groups, start_half, 0)
    rot_copy.wait()
    flips = -(-pairs // max(groups - 1, 1))

    def flip(k):
        for step in range(flips):
            p = jnp.minimum((k - 1) * flips + step, pairs - 1)
            turn[p] = rot[p, 0].astype(F32).T.astype(BF16)

    row_at = lax.broadcasted_iota(jnp.int32, (rows, rank), 0) + row0
    column_at = lax.broadcasted_iota(jnp.int32, (rows, rank), 1)

    def integrate(j, t):
        block = halves[j * sides + t]
        last = j == lanes - 1 and t == sides - 1

        def step(p, carry):
            left = block[orbitals_ref[0, p]]
            right = block[orbitals_ref[1, p]]
            turned = two_parts(dot_nt(turn[p, pl.ds(row0, rows), :], left[:aux]))
            mixed = dot_nn(turned, right[:aux])
            mixed = mixed[:rows] + mixed[rows:]
            if j or t:
                mixed = mixed + integ[p]
            if not last:
                integ[p] = mixed
                return carry
            value = dot_nn(two_parts(mixed), rot[p, 1])
            value = value[:rows] + value[rows:]
            occ = left[aux:].astype(F32)[:1] + right[aux:].astype(F32)[:1]
            first = energies_ref[p][:1]
            second = energies_ref[p][1:]
            first = jnp.sum(jnp.where(row_at == column_at, first, 0.0), axis=1, keepdims=True)
            live = (row_at < ranks_ref[0, p]) & (column_at < ranks_ref[0, p])
            factor = jnp.where(live, -1.0 / (first + second - occ), 0.0)
            integ[p] = value
            scale[p] = factor
            local[p] = (value * factor).astype(BF16)
            return carry

        lax.fori_loop(0, pairs, step, 0, unroll=4 if last else UNROLL)

    finish = spread(0, half_source, half_place, half_place, flip, integrate)
    margin_copy.wait()
    finish()

    def relax(it, p):
        coupled = jnp.zeros((rows, rank), F32)
        for c in range(coups):
            amp = slots[it][:, couplings_ref[c, p]].reshape(rank, rank)
            left = dot_nn(margin[p, c, pl.ds(row0, rows), :], amp).astype(BF16)
            coupled = coupled + weight_ref[c, p] * dot_nt(left, margin[p, c])
        return ((integ[p] - coupled) * scale[p]).astype(BF16)

    def deliver(it):
        e = (it + 1) % 2

        def slot_place(j, t, q):
            index = lax.rem(lane - j + lanes, lanes) * sides + (side if t == 0 else 1 - side)
            return slots[it].at[index, pl.ds(q * capa, capa)]

        def slot_land(j, t, q):
            return slot_place(0 if t == 0 else j, 0, q)

        def slot_source(d):
            return sbuf.at[it, d]

        def post(k, carry):
            to = lax.rem(me + k, groups)
            for s in range(capa):
                sbuf[it, to, s] = local[slots_ref[s, to]]
            group_copy(e, k, slot_source, slot_place).start()
            return carry

        lax.fori_loop(1, groups, post, 0)
        for s in range(capa):
            slots[it][rep, me * capa + s] = local[slots_ref[s, me]]
        return spread(
            e, slot_source, slot_place, slot_land, lambda k: None, lambda j, t: None
        )

    for it in range(ITERS - 1):
        finish = deliver(it)

        def step(p, carry, it=it):
            local[p] = relax(it, p)
            return carry

        lax.fori_loop(0, pairs, step, 0, unroll=UNROLL)
        finish()

    finish = deliver(ITERS - 1)

    def piece(r, chunk):
        return afin.at[r, pl.ds(chunk * share, share)]

    def final_lane(j, chunk):
        block = piece(rep, chunk)
        return send(block, block, fs.at[j, chunk], fr.at[j, chunk], me, lane_rep(j))

    def final_twin(j, chunk):
        block = piece(lane_rep(-j), chunk)
        index = lanes + j
        return send(block, block, fs.at[index, chunk], fr.at[index, chunk], me, twin)

    def relay_final(chunk):
        for j in range(1, lanes):
            block = piece(lane_rep(-j), chunk)
            send(block, block, fs.at[j, chunk], fr.at[j, chunk], me, twin).wait_recv()
            if sides == 2:
                final_twin(j, chunk).start()

    def settle_final(chunk):
        if sides == 2:
            for j in range(lanes):
                other = lax.rem(lane - j + lanes, lanes) * sides + (1 - side)
                block = piece(other, chunk)
                index = lanes + j
                send(block, block, fs.at[index, chunk], fr.at[index, chunk], me, twin).wait_recv()

    def last_chunk(step, carry):
        turn_lane = lax.rem(lane + 1 + step // sides, lanes)
        turn_side = lax.rem(side + step, sides)
        chunk = turn_lane * sides + turn_side
        base = chunk * share
        for k in range(share):
            afin[rep, base + k] = relax(ITERS - 1, base + k)
        for j in range(1, lanes):
            final_lane(j, chunk).start()
        if sides == 2:
            final_twin(0, chunk).start()
        return carry

    lax.fori_loop(0, reps, last_chunk, 0)
    if sides == 2:
        relay_final(twin)
    relay_final(rep)
    settle_final(rep)
    base = rep * share

    def gram(k, carry):
        amp = afin[:, base + k].reshape(rank, rank)
        side_left = dot_nn(rot[base + k, 0], amp).astype(BF16)
        side_right = dot_nt(rot[base + k, 1], amp).astype(BF16)
        grams[2 * k] = dot_nt(side_left, side_left) * (1.0 / rank)
        grams[2 * k + 1] = dot_nt(side_right, side_right) * (1.0 / rank)
        return carry

    lax.fori_loop(0, share, gram, 0, unroll=2)

    def collect(o, carry):
        for r in range(reps):
            span = slice(r * rows, (r + 1) * rows)
            total = jnp.zeros((rows, rank), F32)
            for k in range(share):
                for s in range(2):
                    named = orbitals_ref[s, base + k] == o
                    total = total + jnp.where(named, grams[2 * k + s, span, :], 0.0)
            dsend1[r, o] = total.astype(BF16)
        return carry

    lax.fori_loop(0, norb, collect, 0)

    def density_rep(j):
        to = lax.rem(rep + j, reps)
        return send(dsend1.at[to], drecv1.at[rep], d1s.at[j], d1r.at[j], me, to)

    for j in range(1, reps):
        density_rep(j).start()
    drecv1[rep] = dsend1[rep]

    def rest(step, carry):
        relay_final(lax.rem(lane + step, lanes) * sides + side)
        if sides == 2:
            relay_final(lax.rem(lane + step, lanes) * sides + 1 - side)
        return carry

    lax.fori_loop(1, lanes, rest, 0)
    for j in range(1, reps):
        block = drecv1.at[lax.rem(rep - j + reps, reps)]
        send(block, block, d1s.at[j], d1r.at[j], me, rep).wait_recv()

    def density_group(k):
        to = lax.rem(me + k, groups)
        return send(dsend2.at[to], drecv2.at[me], d2s.at[k], d2r.at[k], to, rep)

    def rep_sum(d):
        total = jnp.zeros((orbs, rows, rank), F32)
        for r in range(reps):
            total = total + drecv1[r, pl.ds(d * orbs, orbs)].astype(F32)
        return total

    def post_density(k, carry):
        to = lax.rem(me + k, groups)
        dsend2[to] = rep_sum(to).astype(BF16)
        density_group(k).start()
        return carry

    lax.fori_loop(1, groups, post_density, 0)
    own = rep_sum(me)

    def take_density(k, total):
        q = lax.rem(me - k + groups, groups)
        block = drecv2.at[q]
        send(block, block, d2s.at[k], d2r.at[k], me, rep).wait_recv()
        return total + drecv2[q].astype(F32)

    dfin[rep] = lax.fori_loop(1, groups, take_density, own)

    def settle_rest(step, carry):
        settle_final(lax.rem(rep + step, reps))
        return carry

    def lay(p, carry):
        for r in range(reps):
            amp_ref[p, r * rows : (r + 1) * rows, :] = afin[r, p]
        return carry

    def density_last(j):
        to = lax.rem(rep + j, reps)
        return send(dfin.at[rep], dfin.at[rep], d3s.at[j], d3r.at[j], me, to)

    for j in range(1, reps):
        density_last(j).start()
    lax.fori_loop(1, reps, settle_rest, 0)
    lax.fori_loop(0, pairs, lay, 0, unroll=4)
    for j in range(1, reps):
        block = dfin.at[lax.rem(rep - j + reps, reps)]
        send(block, block, d3s.at[j], d3r.at[j], me, rep).wait_recv()
    for r in range(reps):
        dens_ref[:, r * rows : (r + 1) * rows, :] = dfin[r]

    finish()
    for chunk in range(reps):
        for j in range(1, lanes):
            final_lane(j, chunk).wait_send()
        if sides == 2:
            for j in range(lanes):
                final_twin(j, chunk).wait_send()
    for j in range(1, reps):
        density_rep(j).wait_send()
        density_last(j).wait_send()

    def sent_density(k, carry):
        density_group(k).wait_send()
        return carry

    lax.fori_loop(1, groups, sent_density, 0)


def body(
    factors,
    orbital_virtuals,
    occupied,
    pair_rotations,
    pair_energies,
    pair_orbitals,
    pair_ranks,
    margins,
    coupling_weight,
    send_slots,
    couplings,
):
    groups = lax.axis_size("pairs")
    reps = lax.axis_size("rep")
    orbs, aux, _ = factors.shape
    pairs, _, rank, _ = pair_rotations.shape
    coups = margins.shape[1]
    capa = send_slots.shape[2]
    rows = rank // reps
    norb = groups * orbs
    share = pairs // reps
    sides = 2 if reps % 2 == 0 else 1
    lanes = reps // sides
    vmem = pl.BlockSpec(memory_space=pltpu.VMEM)
    smem = pl.BlockSpec(memory_space=pltpu.SMEM)
    anywhere = pl.BlockSpec(memory_space=pl.ANY)
    dma = pltpu.SemaphoreType.DMA
    return pl.pallas_call(
        functools.partial(kernel, groups, reps),
        out_shape=(
            jax.ShapeDtypeStruct((pairs, rank, rank), BF16),
            jax.ShapeDtypeStruct((orbs, rank, rank), F32),
        ),
        in_specs=[vmem] * 4 + [smem] * 5 + [anywhere] * 2,
        out_specs=(vmem, vmem),
        scratch_shapes=[
            pltpu.VMEM(pair_rotations.shape, BF16),
            pltpu.VMEM(margins.shape, BF16),
            pltpu.VMEM((pairs, rank, rank), BF16),
            tuple(pltpu.VMEM((norb, aux + OCC_ROWS, rank), BF16) for _ in range(reps)),
            pltpu.VMEM((ITERS, groups, capa, rows, rank), BF16),
            tuple(
                pltpu.VMEM((reps, groups * capa, rows, rank), BF16) for _ in range(ITERS)
            ),
            pltpu.VMEM((pairs, rows, rank), BF16),
            pltpu.VMEM((pairs, rows, rank), F32),
            pltpu.VMEM((pairs, rows, rank), F32),
            pltpu.VMEM((reps, pairs, rows, rank), BF16),
            pltpu.VMEM((2 * share, rank, rank), F32),
            pltpu.VMEM((reps, norb, rows, rank), BF16),
            pltpu.VMEM((reps, norb, rows, rank), BF16),
            pltpu.VMEM((groups, orbs, rows, rank), BF16),
            pltpu.VMEM((groups, orbs, rows, rank), BF16),
            pltpu.VMEM((reps, orbs, rows, rank), F32),
            dma((2,)),
            dma((2, groups)),
            dma((2, groups)),
            dma((2, lanes, groups)),
            dma((2, lanes, groups)),
            dma((2, lanes, groups)),
            dma((2, lanes, groups)),
            dma((2 * lanes, reps)),
            dma((2 * lanes, reps)),
            dma((reps,)),
            dma((reps,)),
            dma((groups,)),
            dma((groups,)),
            dma((reps,)),
            dma((reps,)),
        ],
        compiler_params=pltpu.CompilerParams(
            collective_id=0, has_side_effects=True, vmem_limit_bytes=60 * 1024 * 1024
        ),
        cost_estimate=pl.CostEstimate(
            flops=4 * pairs * coups * ITERS * rows * rank * rank,
            bytes_accessed=2 * pairs * coups * rank * rank,
            transcendentals=0,
        ),
    )(
        factors,
        orbital_virtuals,
        occupied[:, None],
        pair_energies,
        pair_orbitals.T,
        pair_ranks[None, :],
        coupling_weight.T,
        send_slots[0].T,
        couplings.T,
        pair_rotations,
        margins,
    )


def solution(mesh):
    return jax.shard_map(
        body,
        mesh=mesh,
        in_specs=(
            P("pairs", "rep", None),
            P("pairs", None, None),
            P("pairs"),
            P("pairs", None, None, None),
            P("pairs", None, None),
            P("pairs", None),
            P("pairs"),
            P("pairs", None, None, None),
            P("pairs", None),
            P("pairs", None, None),
            P("pairs", None),
        ),
        out_specs=(P("pairs", None, None), P("pairs", None, None)),
        check_vma=False,
    )
```

```python
import functools

import jax
import jax.numpy as jnp
from jax import lax
from jax.experimental import pallas as pl
from jax.experimental.pallas import tpu as pltpu
from jax.sharding import PartitionSpec as P

ITERS = 3
OCC_ROWS = 16
UNROLL = 8
F32 = jnp.float32
BF16 = jnp.bfloat16


def dot_nn(a, b):
    return lax.dot_general(a, b, (((1,), (0,)), ((), ())), preferred_element_type=F32)


def dot_nt(a, b):
    return lax.dot_general(a, b, (((1,), (1,)), ((), ())), preferred_element_type=F32)


def two_parts(x):
    high = x.astype(BF16)
    low = (x - high.astype(F32)).astype(BF16)
    return jnp.concatenate([high, low], axis=0)


def spaced(lhs):
    zero = jnp.zeros_like(lhs[0])
    sides = [[x, zero] if n % 2 == 0 else [zero, x] for n, x in enumerate(lhs)]
    return jnp.concatenate([jnp.concatenate(x, axis=1) for x in sides], axis=0)


def square(a, b, c, d):
    return jnp.concatenate(
        [jnp.concatenate([a, b], axis=1), jnp.concatenate([c, d], axis=1)], axis=0
    )


def apart(out):
    rows, width = out.shape[0] // 4, out.shape[1] // 2
    return [out[n * rows : (n + 1) * rows, (n // 2) * width :][:, :width] for n in range(4)]


def four_nn(lhs, rhs):
    return apart(dot_nn(spaced(lhs), square(rhs[0], rhs[2], rhs[1], rhs[3])))


def four_nt(lhs, rhs):
    return apart(dot_nt(spaced(lhs), square(rhs[0], rhs[1], rhs[2], rhs[3])))


def kernel(
    groups,
    reps,
    factors_ref,
    virtuals_ref,
    occ_ref,
    energies_ref,
    orbitals_ref,
    ranks_ref,
    weight_ref,
    slots_ref,
    couplings_ref,
    rotations_hbm,
    margins_hbm,
    amp_ref,
    dens_ref,
    rot,
    margin,
    turn,
    halves,
    sbuf,
    slots,
    local,
    integ,
    scale,
    afin,
    grams,
    dsend1,
    drecv1,
    dsend2,
    drecv2,
    dfin,
    load_sem,
    s1,
    r1,
    ys,
    yr,
    ss,
    sr,
    fs,
    fr,
    d1s,
    d1r,
    d2s,
    d2r,
    d3s,
    d3r,
):
    me = lax.axis_index("pairs")
    rep = lax.axis_index("rep")
    sides = 2 if reps % 2 == 0 else 1
    lanes = reps // sides
    side = lax.rem(rep, sides)
    lane = rep // sides
    orbs, aux = factors_ref.shape[:2]
    pairs, _, rank, _ = rot.shape
    coups = margin.shape[1]
    rows = rank // reps
    capa = slots_ref.shape[0]
    norb = groups * orbs
    share = pairs // reps
    row0 = pl.multiple_of(rep * rows, rows)

    def lane_rep(step):
        return lax.rem(lane + step + lanes, lanes) * sides + side

    twin = lane * sides + (1 - side)

    def send(src, dst, ssem, rsem, group, to_rep):
        return pltpu.make_async_remote_copy(
            src_ref=src,
            dst_ref=dst,
            send_sem=ssem,
            recv_sem=rsem,
            device_id=(group, to_rep),
            device_id_type=pl.DeviceIdType.MESH,
        )

    rot_copy = pltpu.make_async_copy(rotations_hbm, rot, load_sem.at[0])
    rot_copy.start()
    margin_copy = pltpu.make_async_copy(margins_hbm, margin, load_sem.at[1])
    margin_copy.start()

    barrier = pltpu.get_barrier_semaphore()

    def greet(k, carry):
        pl.semaphore_signal(
            barrier,
            inc=1,
            device_id=(lax.rem(me + k, groups), rep),
            device_id_type=pl.DeviceIdType.MESH,
        )
        return carry

    lax.fori_loop(1, groups, greet, 0)
    for j in range(1, reps):
        pl.semaphore_signal(
            barrier,
            inc=1,
            device_id=(me, lax.rem(rep + j, reps)),
            device_id_type=pl.DeviceIdType.MESH,
        )

    for o in range(orbs):
        half = dot_nn(factors_ref[o], virtuals_ref[o]).astype(BF16)
        level = jnp.broadcast_to(occ_ref[o : o + 1].astype(F32), (OCC_ROWS, rank))
        halves[0][me * orbs + o, :aux, :] = half
        halves[0][me * orbs + o, aux:, :] = level.astype(BF16)

    pl.semaphore_wait(barrier, groups - 1 + reps - 1)

    def group_copy(e, k, src, here):
        to = lax.rem(me + k, groups)
        return send(src(to), here(0, 0, me), s1.at[e, k], r1.at[e, k], to, rep)

    def spread(e, src, here, land, between, ready):
        def source(k):
            return lax.rem(me - k + groups, groups)

        def lane_copy(j, k):
            q = source(k)
            return send(
                here(0, 0, q), land(j, 0, q), ys.at[e, j, k], yr.at[e, j, k], me, lane_rep(j)
            )

        def twin_copy(j, k):
            q = source(k)
            return send(here(j, 0, q), land(j, 1, q), ss.at[e, j, k], sr.at[e, j, k], me, twin)

        def took(place, ssem, rsem):
            send(place, place, ssem, rsem, me, twin).wait_recv()

        def forward(k, carry):
            for j in range(1, lanes):
                lane_copy(j, k).start()
            if sides == 2:
                twin_copy(0, k).start()
            return carry

        def arrive(k, carry):
            between(k)
            took(here(0, 0, source(k)), s1.at[e, k], r1.at[e, k])
            return forward(k, carry)

        forward(0, 0)
        lax.fori_loop(1, groups, arrive, 0)
        ready(0, 0)

        for j in range(1, lanes):

            def relay(k, carry, j=j):
                took(here(j, 0, source(k)), ys.at[e, j, k], yr.at[e, j, k])
                if sides == 2:
                    twin_copy(j, k).start()
                return carry

            lax.fori_loop(0, groups, relay, 0)
            ready(j, 0)

        if sides == 2:
            for j in range(lanes):

                def settle(k, carry, j=j):
                    took(here(j, 1, source(k)), ss.at[e, j, k], sr.at[e, j, k])
                    return carry

                lax.fori_loop(0, groups, settle, 0)
                ready(j, 1)

        def sent(k, carry):
            for j in range(1, lanes):
                lane_copy(j, k).wait_send()
            if sides == 2:
                for j in range(lanes):
                    twin_copy(j, k).wait_send()
            return carry

        def sent_group(k, carry):
            group_copy(e, k, src, here).wait_send()
            return carry

        def finish():
            lax.fori_loop(0, groups, sent, 0)
            lax.fori_loop(1, groups, sent_group, 0)

        return finish

    def half_place(j, t, q):
        return halves[j * sides + t].at[pl.ds(q * orbs, orbs)]

    def half_source(d):
        return half_place(0, 0, me)

    def start_half(k, carry):
        group_copy(0, k, half_source, half_place).start()
        return carry

    lax.fori_loop(1, groups, start_half, 0)
    rot_copy.wait()
    flips = -(-pairs // max(groups - 1, 1))

    def flip(k):
        for step in range(flips):
            p = jnp.minimum((k - 1) * flips + step, pairs - 1)
            turn[p] = rot[p, 0].astype(F32).T.astype(BF16)

    row_at = lax.broadcasted_iota(jnp.int32, (rows, rank), 0) + row0
    column_at = lax.broadcasted_iota(jnp.int32, (rows, rank), 1)

    def integrate(j, t):
        block = halves[j * sides + t]
        last = j == lanes - 1 and t == sides - 1

        def step(n, carry):
            four = [4 * n + m for m in range(4)]
            left = [block[orbitals_ref[0, p]] for p in four]
            right = [block[orbitals_ref[1, p]] for p in four]
            turned = four_nt(
                [turn[p, pl.ds(row0, rows), :] for p in four], [x[:aux] for x in left]
            )
            mixed = four_nn([two_parts(x) for x in turned], [x[:aux] for x in right])
            mixed = [x[:rows] + x[rows:] for x in mixed]
            if j or t:
                mixed = [x + integ[p] for x, p in zip(mixed, four)]
            if not last:
                for x, p in zip(mixed, four):
                    integ[p] = x
                return carry
            values = four_nn([two_parts(x) for x in mixed], [rot[p, 1] for p in four])
            for m, p in enumerate(four):
                value = values[m][:rows] + values[m][rows:]
                occ = left[m][aux:].astype(F32)[:1] + right[m][aux:].astype(F32)[:1]
                first = energies_ref[p][:1]
                second = energies_ref[p][1:]
                first = jnp.sum(jnp.where(row_at == column_at, first, 0.0), axis=1, keepdims=True)
                live = (row_at < ranks_ref[0, p]) & (column_at < ranks_ref[0, p])
                factor = jnp.where(live, -1.0 / (first + second - occ), 0.0)
                integ[p] = value
                scale[p] = factor
                local[p] = (value * factor).astype(BF16)
            return carry

        lax.fori_loop(0, pairs // 4, step, 0, unroll=2)

    finish = spread(0, half_source, half_place, half_place, flip, integrate)
    margin_copy.wait()
    finish()

    def relax(it, p):
        items = [(p + n, c) for n in range(2) for c in range(coups)]
        lefts = []
        for at in range(0, len(items), 4):
            four = items[at : at + 4]
            got = four_nn(
                [margin[n, c, pl.ds(row0, rows), :] for n, c in four],
                [slots[it][:, couplings_ref[c, n]].reshape(rank, rank) for n, c in four],
            )
            lefts += [(weight_ref[c, n] * x).astype(BF16) for (n, c), x in zip(four, got)]
        two = [jnp.concatenate(lefts[n * coups : (n + 1) * coups], axis=1) for n in range(2)]
        wide = [
            jnp.concatenate([margin[p + n, c] for c in range(coups)], axis=1) for n in range(2)
        ]
        coupled = dot_nt(jnp.concatenate(two, axis=0), jnp.concatenate(wide, axis=0))
        parts = (coupled[:rows, :rank], coupled[rows:, rank:])
        return [
            ((integ[p + n] - parts[n]) * scale[p + n]).astype(BF16) for n in range(2)
        ]

    def deliver(it):
        e = (it + 1) % 2

        def slot_place(j, t, q):
            index = lax.rem(lane - j + lanes, lanes) * sides + (side if t == 0 else 1 - side)
            return slots[it].at[index, pl.ds(q * capa, capa)]

        def slot_land(j, t, q):
            return slot_place(0 if t == 0 else j, 0, q)

        def slot_source(d):
            return sbuf.at[it, d]

        def post(k, carry):
            to = lax.rem(me + k, groups)
            for s in range(capa):
                sbuf[it, to, s] = local[slots_ref[s, to]]
            group_copy(e, k, slot_source, slot_place).start()
            return carry

        lax.fori_loop(1, groups, post, 0)
        for s in range(capa):
            slots[it][rep, me * capa + s] = local[slots_ref[s, me]]
        return spread(
            e, slot_source, slot_place, slot_land, lambda k: None, lambda j, t: None
        )

    for it in range(ITERS - 1):
        finish = deliver(it)

        def step(n, carry, it=it):
            local[2 * n], local[2 * n + 1] = relax(it, 2 * n)
            return carry

        lax.fori_loop(0, pairs // 2, step, 0, unroll=UNROLL // 2)
        finish()

    finish = deliver(ITERS - 1)

    def piece(r, chunk):
        return afin.at[r, pl.ds(chunk * share, share)]

    def final_lane(j, chunk):
        block = piece(rep, chunk)
        return send(block, block, fs.at[j, chunk], fr.at[j, chunk], me, lane_rep(j))

    def final_twin(j, chunk):
        block = piece(lane_rep(-j), chunk)
        index = lanes + j
        return send(block, block, fs.at[index, chunk], fr.at[index, chunk], me, twin)

    def relay_final(chunk):
        for j in range(1, lanes):
            block = piece(lane_rep(-j), chunk)
            send(block, block, fs.at[j, chunk], fr.at[j, chunk], me, twin).wait_recv()
            if sides == 2:
                final_twin(j, chunk).start()

    def settle_final(chunk):
        if sides == 2:
            for j in range(lanes):
                other = lax.rem(lane - j + lanes, lanes) * sides + (1 - side)
                block = piece(other, chunk)
                index = lanes + j
                send(block, block, fs.at[index, chunk], fr.at[index, chunk], me, twin).wait_recv()

    def last_chunk(step, carry):
        turn_lane = lax.rem(lane + 1 + step // sides, lanes)
        turn_side = lax.rem(side + step, sides)
        chunk = turn_lane * sides + turn_side
        base = chunk * share
        for k in range(0, share, 2):
            afin[rep, base + k], afin[rep, base + k + 1] = relax(ITERS - 1, base + k)
        for j in range(1, lanes):
            final_lane(j, chunk).start()
        if sides == 2:
            final_twin(0, chunk).start()
        return carry

    lax.fori_loop(0, reps, last_chunk, 0)
    if sides == 2:
        relay_final(twin)
    relay_final(rep)
    settle_final(rep)
    base = rep * share

    def gram(k, carry):
        amp = afin[:, base + k].reshape(rank, rank)
        side_left = dot_nn(rot[base + k, 0], amp).astype(BF16)
        side_right = dot_nt(rot[base + k, 1], amp).astype(BF16)
        grams[2 * k] = dot_nt(side_left, side_left) * (1.0 / rank)
        grams[2 * k + 1] = dot_nt(side_right, side_right) * (1.0 / rank)
        return carry

    lax.fori_loop(0, share, gram, 0, unroll=2)

    def collect(o, carry):
        for r in range(reps):
            span = slice(r * rows, (r + 1) * rows)
            total = jnp.zeros((rows, rank), F32)
            for k in range(share):
                for s in range(2):
                    named = orbitals_ref[s, base + k] == o
                    total = total + jnp.where(named, grams[2 * k + s, span, :], 0.0)
            dsend1[r, o] = total.astype(BF16)
        return carry

    lax.fori_loop(0, norb, collect, 0)

    def density_rep(j):
        to = lax.rem(rep + j, reps)
        return send(dsend1.at[to], drecv1.at[rep], d1s.at[j], d1r.at[j], me, to)

    for j in range(1, reps):
        density_rep(j).start()
    drecv1[rep] = dsend1[rep]

    def rest(step, carry):
        relay_final(lax.rem(lane + step, lanes) * sides + side)
        if sides == 2:
            relay_final(lax.rem(lane + step, lanes) * sides + 1 - side)
        return carry

    lax.fori_loop(1, lanes, rest, 0)
    for j in range(1, reps):
        block = drecv1.at[lax.rem(rep - j + reps, reps)]
        send(block, block, d1s.at[j], d1r.at[j], me, rep).wait_recv()

    def density_group(k):
        to = lax.rem(me + k, groups)
        return send(dsend2.at[to], drecv2.at[me], d2s.at[k], d2r.at[k], to, rep)

    def rep_sum(d):
        total = jnp.zeros((orbs, rows, rank), F32)
        for r in range(reps):
            total = total + drecv1[r, pl.ds(d * orbs, orbs)].astype(F32)
        return total

    def post_density(k, carry):
        to = lax.rem(me + k, groups)
        dsend2[to] = rep_sum(to).astype(BF16)
        density_group(k).start()
        return carry

    lax.fori_loop(1, groups, post_density, 0)
    own = rep_sum(me)

    def take_density(k, total):
        q = lax.rem(me - k + groups, groups)
        block = drecv2.at[q]
        send(block, block, d2s.at[k], d2r.at[k], me, rep).wait_recv()
        return total + drecv2[q].astype(F32)

    dfin[rep] = lax.fori_loop(1, groups, take_density, own)

    def settle_rest(step, carry):
        settle_final(lax.rem(rep + step, reps))
        return carry

    def lay(p, carry):
        for r in range(reps):
            amp_ref[p, r * rows : (r + 1) * rows, :] = afin[r, p]
        return carry

    def density_last(j):
        to = lax.rem(rep + j, reps)
        return send(dfin.at[rep], dfin.at[rep], d3s.at[j], d3r.at[j], me, to)

    for j in range(1, reps):
        density_last(j).start()
    lax.fori_loop(1, reps, settle_rest, 0)
    lax.fori_loop(0, pairs, lay, 0, unroll=4)
    for j in range(1, reps):
        block = dfin.at[lax.rem(rep - j + reps, reps)]
        send(block, block, d3s.at[j], d3r.at[j], me, rep).wait_recv()
    for r in range(reps):
        dens_ref[:, r * rows : (r + 1) * rows, :] = dfin[r]

    finish()
    for chunk in range(reps):
        for j in range(1, lanes):
            final_lane(j, chunk).wait_send()
        if sides == 2:
            for j in range(lanes):
                final_twin(j, chunk).wait_send()
    for j in range(1, reps):
        density_rep(j).wait_send()
        density_last(j).wait_send()

    def sent_density(k, carry):
        density_group(k).wait_send()
        return carry

    lax.fori_loop(1, groups, sent_density, 0)


def body(
    factors,
    orbital_virtuals,
    occupied,
    pair_rotations,
    pair_energies,
    pair_orbitals,
    pair_ranks,
    margins,
    coupling_weight,
    send_slots,
    couplings,
):
    groups = lax.axis_size("pairs")
    reps = lax.axis_size("rep")
    orbs, aux, _ = factors.shape
    pairs, _, rank, _ = pair_rotations.shape
    coups = margins.shape[1]
    capa = send_slots.shape[2]
    rows = rank // reps
    norb = groups * orbs
    share = pairs // reps
    sides = 2 if reps % 2 == 0 else 1
    lanes = reps // sides
    vmem = pl.BlockSpec(memory_space=pltpu.VMEM)
    smem = pl.BlockSpec(memory_space=pltpu.SMEM)
    anywhere = pl.BlockSpec(memory_space=pl.ANY)
    dma = pltpu.SemaphoreType.DMA
    return pl.pallas_call(
        functools.partial(kernel, groups, reps),
        out_shape=(
            jax.ShapeDtypeStruct((pairs, rank, rank), BF16),
            jax.ShapeDtypeStruct((orbs, rank, rank), F32),
        ),
        in_specs=[vmem] * 4 + [smem] * 5 + [anywhere] * 2,
        out_specs=(vmem, vmem),
        scratch_shapes=[
            pltpu.VMEM(pair_rotations.shape, BF16),
            pltpu.VMEM(margins.shape, BF16),
            pltpu.VMEM((pairs, rank, rank), BF16),
            tuple(pltpu.VMEM((norb, aux + OCC_ROWS, rank), BF16) for _ in range(reps)),
            pltpu.VMEM((ITERS, groups, capa, rows, rank), BF16),
            tuple(
                pltpu.VMEM((reps, groups * capa, rows, rank), BF16) for _ in range(ITERS)
            ),
            pltpu.VMEM((pairs, rows, rank), BF16),
            pltpu.VMEM((pairs, rows, rank), F32),
            pltpu.VMEM((pairs, rows, rank), F32),
            pltpu.VMEM((reps, pairs, rows, rank), BF16),
            pltpu.VMEM((2 * share, rank, rank), F32),
            pltpu.VMEM((reps, norb, rows, rank), BF16),
            pltpu.VMEM((reps, norb, rows, rank), BF16),
            pltpu.VMEM((groups, orbs, rows, rank), BF16),
            pltpu.VMEM((groups, orbs, rows, rank), BF16),
            pltpu.VMEM((reps, orbs, rows, rank), F32),
            dma((2,)),
            dma((2, groups)),
            dma((2, groups)),
            dma((2, lanes, groups)),
            dma((2, lanes, groups)),
            dma((2, lanes, groups)),
            dma((2, lanes, groups)),
            dma((2 * lanes, reps)),
            dma((2 * lanes, reps)),
            dma((reps,)),
            dma((reps,)),
            dma((groups,)),
            dma((groups,)),
            dma((reps,)),
            dma((reps,)),
        ],
        compiler_params=pltpu.CompilerParams(
            collective_id=0, has_side_effects=True, vmem_limit_bytes=60 * 1024 * 1024
        ),
        cost_estimate=pl.CostEstimate(
            flops=4 * pairs * coups * ITERS * rows * rank * rank,
            bytes_accessed=2 * pairs * coups * rank * rank,
            transcendentals=0,
        ),
    )(
        factors,
        orbital_virtuals,
        occupied[:, None],
        pair_energies,
        pair_orbitals.T,
        pair_ranks[None, :],
        coupling_weight.T,
        send_slots[0].T,
        couplings.T,
        pair_rotations,
        margins,
    )


def solution(mesh):
    return jax.shard_map(
        body,
        mesh=mesh,
        in_specs=(
            P("pairs", "rep", None),
            P("pairs", None, None),
            P("pairs"),
            P("pairs", None, None, None),
            P("pairs", None, None),
            P("pairs", None),
            P("pairs"),
            P("pairs", None, None, None),
            P("pairs", None),
            P("pairs", None, None),
            P("pairs", None),
        ),
        out_specs=(P("pairs", None, None), P("pairs", None, None)),
        check_vma=False,
    )
```

```python
import functools

import jax
import jax.numpy as jnp
from jax import lax
from jax.experimental import pallas as pl
from jax.experimental.pallas import tpu as pltpu
from jax.sharding import PartitionSpec as P

ITERS = 3
OCC_ROWS = 16
UNROLL = 8
HALF_PARTS = 4
SLOT_PARTS = 2
F32 = jnp.float32
BF16 = jnp.bfloat16


def dot_nn(a, b):
    return lax.dot_general(a, b, (((1,), (0,)), ((), ())), preferred_element_type=F32)


def dot_nt(a, b):
    return lax.dot_general(a, b, (((1,), (1,)), ((), ())), preferred_element_type=F32)


def two_parts(x):
    high = x.astype(BF16)
    low = (x - high.astype(F32)).astype(BF16)
    return jnp.concatenate([high, low], axis=0)


def spaced(lhs):
    zero = jnp.zeros_like(lhs[0])
    sides = [[x, zero] if n % 2 == 0 else [zero, x] for n, x in enumerate(lhs)]
    return jnp.concatenate([jnp.concatenate(x, axis=1) for x in sides], axis=0)


def square(a, b, c, d):
    return jnp.concatenate(
        [jnp.concatenate([a, b], axis=1), jnp.concatenate([c, d], axis=1)], axis=0
    )


def apart(out):
    rows, width = out.shape[0] // 4, out.shape[1] // 2
    return [out[n * rows : (n + 1) * rows, (n // 2) * width :][:, :width] for n in range(4)]


def four_nn(lhs, rhs):
    return apart(dot_nn(spaced(lhs), square(rhs[0], rhs[2], rhs[1], rhs[3])))


def four_nt(lhs, rhs):
    return apart(dot_nt(spaced(lhs), square(rhs[0], rhs[1], rhs[2], rhs[3])))


def kernel(
    groups,
    reps,
    factors_ref,
    virtuals_ref,
    occ_ref,
    energies_ref,
    orbitals_ref,
    ranks_ref,
    weight_ref,
    slots_ref,
    couplings_ref,
    rotations_hbm,
    margins_hbm,
    amp_hbm,
    dens_ref,
    rot,
    margin,
    turn,
    halves,
    sbuf,
    slots,
    local,
    integ,
    scale,
    afin,
    grams,
    dsend1,
    drecv1,
    dsend2,
    drecv2,
    dfin,
    load_sem,
    lay_sem,
    s1,
    r1,
    ys,
    yr,
    ss,
    sr,
    fs,
    fr,
    d1s,
    d1r,
    d2s,
    d2r,
    d3s,
    d3r,
):
    me = lax.axis_index("pairs")
    rep = lax.axis_index("rep")
    sides = 2 if reps % 2 == 0 else 1
    lanes = reps // sides
    side = lax.rem(rep, sides)
    lane = rep // sides
    orbs, aux = factors_ref.shape[:2]
    pairs, _, rank, _ = rot.shape
    coups = margin.shape[1]
    rows = rank // reps
    capa = slots_ref.shape[0]
    norb = groups * orbs
    share = pairs // reps
    row0 = pl.multiple_of(rep * rows, rows)

    def lane_rep(step):
        return lax.rem(lane + step + lanes, lanes) * sides + side

    twin = lane * sides + (1 - side)

    def send(src, dst, ssem, rsem, group, to_rep):
        return pltpu.make_async_remote_copy(
            src_ref=src,
            dst_ref=dst,
            send_sem=ssem,
            recv_sem=rsem,
            device_id=(group, to_rep),
            device_id_type=pl.DeviceIdType.MESH,
        )

    rot_copy = pltpu.make_async_copy(rotations_hbm, rot, load_sem.at[0])
    rot_copy.start()
    margin_copy = pltpu.make_async_copy(margins_hbm, margin, load_sem.at[1])
    margin_copy.start()

    barrier = pltpu.get_barrier_semaphore()

    def greet(k, carry):
        pl.semaphore_signal(
            barrier,
            inc=1,
            device_id=(lax.rem(me + k, groups), rep),
            device_id_type=pl.DeviceIdType.MESH,
        )
        return carry

    lax.fori_loop(1, groups, greet, 0)
    for j in range(1, reps):
        pl.semaphore_signal(
            barrier,
            inc=1,
            device_id=(me, lax.rem(rep + j, reps)),
            device_id_type=pl.DeviceIdType.MESH,
        )

    for o in range(orbs):
        half = dot_nn(factors_ref[o], virtuals_ref[o]).astype(BF16)
        level = jnp.broadcast_to(occ_ref[o : o + 1].astype(F32), (OCC_ROWS, rank))
        halves[0][o, :aux, :] = half
        halves[0][o, aux:, :] = level.astype(BF16)

    pl.semaphore_wait(barrier, groups - 1 + reps - 1)

    def group_copy(e, k, src, here):
        to = lax.rem(me + k, groups)
        return send(src(to), here(0, 0, k, 1), s1.at[e, k], r1.at[e, k], to, rep)

    def nearness(index, width):
        within = lax.rem(index, width)
        return lax.rem(width * (me + groups) - (index - within), width * groups) + within

    def spread(e, src, here, land, parts, between, ready):
        parts = parts if groups % parts == 0 else 1
        size = groups // parts

        def lane_copy(j, n):
            k = n * size
            return send(
                here(0, 0, k, size),
                land(j, 0, k, size),
                ys.at[e, j, n],
                yr.at[e, j, n],
                me,
                lane_rep(j),
            )

        def twin_copy(j, n):
            k = n * size
            return send(
                here(j, 0, k, size), land(j, 1, k, size), ss.at[e, j, n], sr.at[e, j, n], me, twin
            )

        def took(place, ssem, rsem):
            send(place, place, ssem, rsem, me, twin).wait_recv()

        def arrive(k, carry):
            between(k)
            took(here(0, 0, k, 1), s1.at[e, k], r1.at[e, k])
            return carry

        for n in range(parts):
            lax.fori_loop(max(n * size, 1), (n + 1) * size, arrive, 0)
            for j in range(1, lanes):
                lane_copy(j, n).start()
            if sides == 2:
                twin_copy(0, n).start()
        ready(0, 0)

        for j in range(1, lanes):
            for n in range(parts):
                took(here(j, 0, n * size, size), ys.at[e, j, n], yr.at[e, j, n])
                if sides == 2:
                    twin_copy(j, n).start()
            ready(j, 0)

        if sides == 2:
            for j in range(lanes):
                for n in range(parts):
                    took(here(j, 1, n * size, size), ss.at[e, j, n], sr.at[e, j, n])
                ready(j, 1)

        def sent_group(k, carry):
            group_copy(e, k, src, here).wait_send()
            return carry

        def finish():
            for n in range(parts):
                for j in range(1, lanes):
                    lane_copy(j, n).wait_send()
                if sides == 2:
                    for j in range(lanes):
                        twin_copy(j, n).wait_send()
            lax.fori_loop(1, groups, sent_group, 0)

        return finish

    def half_place(j, t, k, n):
        return halves[j * sides + t].at[pl.ds(k * orbs, n * orbs)]

    def half_source(d):
        return half_place(0, 0, 0, 1)

    def start_half(k, carry):
        group_copy(0, k, half_source, half_place).start()
        return carry

    lax.fori_loop(1, groups, start_half, 0)
    rot_copy.wait()
    flips = -(-pairs // max(groups - 1, 1))

    def flip(k):
        for step in range(flips):
            p = jnp.minimum((k - 1) * flips + step, pairs - 1)
            turn[p] = rot[p, 0].astype(F32).T.astype(BF16)

    row_at = lax.broadcasted_iota(jnp.int32, (rows, rank), 0) + row0
    column_at = lax.broadcasted_iota(jnp.int32, (rows, rank), 1)

    def integrate(j, t):
        block = halves[j * sides + t]
        last = j == lanes - 1 and t == sides - 1

        def step(n, carry):
            four = [4 * n + m for m in range(4)]
            left = [block[nearness(orbitals_ref[0, p], orbs)] for p in four]
            right = [block[nearness(orbitals_ref[1, p], orbs)] for p in four]
            turned = four_nt(
                [turn[p, pl.ds(row0, rows), :] for p in four], [x[:aux] for x in left]
            )
            mixed = four_nn([two_parts(x) for x in turned], [x[:aux] for x in right])
            mixed = [x[:rows] + x[rows:] for x in mixed]
            if j or t:
                mixed = [x + integ[p] for x, p in zip(mixed, four)]
            if not last:
                for x, p in zip(mixed, four):
                    integ[p] = x
                return carry
            values = four_nn([two_parts(x) for x in mixed], [rot[p, 1] for p in four])
            for m, p in enumerate(four):
                value = values[m][:rows] + values[m][rows:]
                occ = left[m][aux:].astype(F32)[:1] + right[m][aux:].astype(F32)[:1]
                first = energies_ref[p][:1]
                second = energies_ref[p][1:]
                first = jnp.sum(jnp.where(row_at == column_at, first, 0.0), axis=1, keepdims=True)
                live = (row_at < ranks_ref[0, p]) & (column_at < ranks_ref[0, p])
                factor = jnp.where(live, -1.0 / (first + second - occ), 0.0)
                integ[p] = value
                scale[p] = factor
                local[p] = (value * factor).astype(BF16)
            return carry

        lax.fori_loop(0, pairs // 4, step, 0, unroll=2)

    finish = spread(0, half_source, half_place, half_place, HALF_PARTS, flip, integrate)
    margin_copy.wait()
    finish()

    def relax(it, p):
        items = [(p + n, c) for n in range(2) for c in range(coups)]
        lefts = []
        for at in range(0, len(items), 4):
            four = items[at : at + 4]
            got = four_nn(
                [margin[n, c, pl.ds(row0, rows), :] for n, c in four],
                [
                    slots[it][:, nearness(couplings_ref[c, n], capa)].reshape(rank, rank)
                    for n, c in four
                ],
            )
            lefts += [(weight_ref[c, n] * x).astype(BF16) for (n, c), x in zip(four, got)]
        two = [jnp.concatenate(lefts[n * coups : (n + 1) * coups], axis=1) for n in range(2)]
        wide = [
            jnp.concatenate([margin[p + n, c] for c in range(coups)], axis=1) for n in range(2)
        ]
        coupled = dot_nt(jnp.concatenate(two, axis=0), jnp.concatenate(wide, axis=0))
        parts = (coupled[:rows, :rank], coupled[rows:, rank:])
        return [
            ((integ[p + n] - parts[n]) * scale[p + n]).astype(BF16) for n in range(2)
        ]

    def deliver(it):
        e = (it + 1) % 2

        def slot_place(j, t, k, n):
            index = lax.rem(lane - j + lanes, lanes) * sides + (side if t == 0 else 1 - side)
            return slots[it].at[index, pl.ds(k * capa, n * capa)]

        def slot_land(j, t, k, n):
            return slot_place(0 if t == 0 else j, 0, k, n)

        def slot_source(d):
            return sbuf.at[it, d]

        def post(k, carry):
            to = lax.rem(me + k, groups)
            for s in range(capa):
                sbuf[it, to, s] = local[slots_ref[s, to]]
            group_copy(e, k, slot_source, slot_place).start()
            return carry

        lax.fori_loop(1, groups, post, 0)
        for s in range(capa):
            slots[it][rep, s] = local[slots_ref[s, me]]
        return spread(
            e,
            slot_source,
            slot_place,
            slot_land,
            SLOT_PARTS,
            lambda k: None,
            lambda j, t: None,
        )

    for it in range(ITERS - 1):
        finish = deliver(it)

        def step(n, carry, it=it):
            local[2 * n], local[2 * n + 1] = relax(it, 2 * n)
            return carry

        lax.fori_loop(0, pairs // 2, step, 0, unroll=UNROLL // 2)
        finish()

    finish = deliver(ITERS - 1)

    def piece(r, chunk):
        return afin.at[r, pl.ds(chunk * share, share)]

    def final_lane(j, chunk):
        block = piece(rep, chunk)
        return send(block, block, fs.at[j, chunk], fr.at[j, chunk], me, lane_rep(j))

    def final_twin(j, chunk):
        block = piece(lane_rep(-j), chunk)
        index = lanes + j
        return send(block, block, fs.at[index, chunk], fr.at[index, chunk], me, twin)

    def relay_final(chunk):
        for j in range(1, lanes):
            block = piece(lane_rep(-j), chunk)
            send(block, block, fs.at[j, chunk], fr.at[j, chunk], me, twin).wait_recv()
            if sides == 2:
                final_twin(j, chunk).start()

    def settle_final(chunk):
        if sides == 2:
            for j in range(lanes):
                other = lax.rem(lane - j + lanes, lanes) * sides + (1 - side)
                block = piece(other, chunk)
                index = lanes + j
                send(block, block, fs.at[index, chunk], fr.at[index, chunk], me, twin).wait_recv()

    def last_chunk(step, carry):
        turn_lane = lax.rem(lane + 1 + step // sides, lanes)
        turn_side = lax.rem(side + step, sides)
        chunk = turn_lane * sides + turn_side
        base = chunk * share
        for k in range(0, share, 2):
            afin[rep, base + k], afin[rep, base + k + 1] = relax(ITERS - 1, base + k)
        for j in range(1, lanes):
            final_lane(j, chunk).start()
        if sides == 2:
            final_twin(0, chunk).start()
        return carry

    lax.fori_loop(0, reps, last_chunk, 0)
    if sides == 2:
        relay_final(twin)
    relay_final(rep)
    settle_final(rep)
    base = rep * share

    def gram(n, carry):
        four = [4 * n + m for m in range(4)]
        amps = [afin[:, base + k].reshape(rank, rank) for k in four]
        left = four_nn([rot[base + k, 0] for k in four], amps)
        right = four_nt([rot[base + k, 1] for k in four], amps)
        for s, sides_of in enumerate((left, right)):
            rounded = [x.astype(BF16) for x in sides_of]
            for k, x in zip(four, four_nt(rounded, rounded)):
                grams[2 * k + s] = x * (1.0 / rank)
        return carry

    lax.fori_loop(0, share // 4, gram, 0, unroll=2)

    def collect(o, carry):
        for r in range(reps):
            span = slice(r * rows, (r + 1) * rows)
            total = jnp.zeros((rows, rank), F32)
            for k in range(share):
                for s in range(2):
                    named = orbitals_ref[s, base + k] == o
                    total = total + jnp.where(named, grams[2 * k + s, span, :], 0.0)
            dsend1[r, o] = total.astype(BF16)
        return carry

    lax.fori_loop(0, norb, collect, 0)

    def density_rep(j):
        to = lax.rem(rep + j, reps)
        return send(dsend1.at[to], drecv1.at[rep], d1s.at[j], d1r.at[j], me, to)

    for j in range(1, reps):
        density_rep(j).start()
    drecv1[rep] = dsend1[rep]

    def rest(step, carry):
        relay_final(lax.rem(lane + step, lanes) * sides + side)
        if sides == 2:
            relay_final(lax.rem(lane + step, lanes) * sides + 1 - side)
        return carry

    lax.fori_loop(1, lanes, rest, 0)
    for j in range(1, reps):
        block = drecv1.at[lax.rem(rep - j + reps, reps)]
        send(block, block, d1s.at[j], d1r.at[j], me, rep).wait_recv()

    def density_group(k):
        to = lax.rem(me + k, groups)
        return send(dsend2.at[to], drecv2.at[me], d2s.at[k], d2r.at[k], to, rep)

    def rep_sum(d):
        total = jnp.zeros((orbs, rows, rank), F32)
        for r in range(reps):
            total = total + drecv1[r, pl.ds(d * orbs, orbs)].astype(F32)
        return total

    def post_density(k, carry):
        to = lax.rem(me + k, groups)
        dsend2[to] = rep_sum(to).astype(BF16)
        density_group(k).start()
        return carry

    lax.fori_loop(1, groups, post_density, 0)
    own = rep_sum(me)

    def take_density(k, total):
        q = lax.rem(me - k + groups, groups)
        block = drecv2.at[q]
        send(block, block, d2s.at[k], d2r.at[k], me, rep).wait_recv()
        return total + drecv2[q].astype(F32)

    dfin[rep] = lax.fori_loop(1, groups, take_density, own)

    def settle_rest(step, carry):
        settle_final(lax.rem(rep + step, reps))
        return carry

    def lay(r):
        return pltpu.make_async_copy(
            afin.at[r], amp_hbm.at[:, pl.ds(r * rows, rows), :], lay_sem.at[r]
        )

    def density_last(j):
        to = lax.rem(rep + j, reps)
        return send(dfin.at[rep], dfin.at[rep], d3s.at[j], d3r.at[j], me, to)

    for j in range(1, reps):
        density_last(j).start()
    lax.fori_loop(1, reps, settle_rest, 0)
    for r in range(reps):
        lay(r).start()
    for j in range(1, reps):
        block = dfin.at[lax.rem(rep - j + reps, reps)]
        send(block, block, d3s.at[j], d3r.at[j], me, rep).wait_recv()
    for r in range(reps):
        dens_ref[:, r * rows : (r + 1) * rows, :] = dfin[r]

    finish()
    for r in range(reps):
        lay(r).wait()
    for chunk in range(reps):
        for j in range(1, lanes):
            final_lane(j, chunk).wait_send()
        if sides == 2:
            for j in range(lanes):
                final_twin(j, chunk).wait_send()
    for j in range(1, reps):
        density_rep(j).wait_send()
        density_last(j).wait_send()

    def sent_density(k, carry):
        density_group(k).wait_send()
        return carry

    lax.fori_loop(1, groups, sent_density, 0)


def body(
    factors,
    orbital_virtuals,
    occupied,
    pair_rotations,
    pair_energies,
    pair_orbitals,
    pair_ranks,
    margins,
    coupling_weight,
    send_slots,
    couplings,
):
    groups = lax.axis_size("pairs")
    reps = lax.axis_size("rep")
    orbs, aux, _ = factors.shape
    pairs, _, rank, _ = pair_rotations.shape
    coups = margins.shape[1]
    capa = send_slots.shape[2]
    rows = rank // reps
    norb = groups * orbs
    share = pairs // reps
    sides = 2 if reps % 2 == 0 else 1
    lanes = reps // sides
    vmem = pl.BlockSpec(memory_space=pltpu.VMEM)
    smem = pl.BlockSpec(memory_space=pltpu.SMEM)
    anywhere = pl.BlockSpec(memory_space=pl.ANY)
    dma = pltpu.SemaphoreType.DMA
    return pl.pallas_call(
        functools.partial(kernel, groups, reps),
        out_shape=(
            jax.ShapeDtypeStruct((pairs, rank, rank), BF16),
            jax.ShapeDtypeStruct((orbs, rank, rank), F32),
        ),
        in_specs=[vmem] * 4 + [smem] * 5 + [anywhere] * 2,
        out_specs=(anywhere, vmem),
        scratch_shapes=[
            pltpu.VMEM(pair_rotations.shape, BF16),
            pltpu.VMEM(margins.shape, BF16),
            pltpu.VMEM((pairs, rank, rank), BF16),
            tuple(pltpu.VMEM((norb, aux + OCC_ROWS, rank), BF16) for _ in range(reps)),
            pltpu.VMEM((ITERS, groups, capa, rows, rank), BF16),
            tuple(
                pltpu.VMEM((reps, groups * capa, rows, rank), BF16) for _ in range(ITERS)
            ),
            pltpu.VMEM((pairs, rows, rank), BF16),
            pltpu.VMEM((pairs, rows, rank), F32),
            pltpu.VMEM((pairs, rows, rank), F32),
            pltpu.VMEM((reps, pairs, rows, rank), BF16),
            pltpu.VMEM((2 * share, rank, rank), F32),
            pltpu.VMEM((reps, norb, rows, rank), BF16),
            pltpu.VMEM((reps, norb, rows, rank), BF16),
            pltpu.VMEM((groups, orbs, rows, rank), BF16),
            pltpu.VMEM((groups, orbs, rows, rank), BF16),
            pltpu.VMEM((reps, orbs, rows, rank), F32),
            dma((2,)),
            dma((reps,)),
            dma((2, groups)),
            dma((2, groups)),
            dma((2, lanes, max(HALF_PARTS, SLOT_PARTS))),
            dma((2, lanes, max(HALF_PARTS, SLOT_PARTS))),
            dma((2, lanes, max(HALF_PARTS, SLOT_PARTS))),
            dma((2, lanes, max(HALF_PARTS, SLOT_PARTS))),
            dma((2 * lanes, reps)),
            dma((2 * lanes, reps)),
            dma((reps,)),
            dma((reps,)),
            dma((groups,)),
            dma((groups,)),
            dma((reps,)),
            dma((reps,)),
        ],
        compiler_params=pltpu.CompilerParams(
            collective_id=0, has_side_effects=True, vmem_limit_bytes=60 * 1024 * 1024
        ),
        cost_estimate=pl.CostEstimate(
            flops=4 * pairs * coups * ITERS * rows * rank * rank,
            bytes_accessed=2 * pairs * coups * rank * rank,
            transcendentals=0,
        ),
    )(
        factors,
        orbital_virtuals,
        occupied[:, None],
        pair_energies,
        pair_orbitals.T,
        pair_ranks[None, :],
        coupling_weight.T,
        send_slots[0].T,
        couplings.T,
        pair_rotations,
        margins,
    )


def solution(mesh):
    return jax.shard_map(
        body,
        mesh=mesh,
        in_specs=(
            P("pairs", "rep", None),
            P("pairs", None, None),
            P("pairs"),
            P("pairs", None, None, None),
            P("pairs", None, None),
            P("pairs", None),
            P("pairs"),
            P("pairs", None, None, None),
            P("pairs", None),
            P("pairs", None, None),
            P("pairs", None),
        ),
        out_specs=(P("pairs", None, None), P("pairs", None, None)),
        check_vma=False,
    )
```

```python
import functools

import jax
import jax.numpy as jnp
from jax import lax
from jax.experimental import pallas as pl
from jax.experimental.pallas import tpu as pltpu
from jax.sharding import PartitionSpec as P

ITERS = 3
OCC_ROWS = 16
UNROLL = 8
HALF_PARTS = 8
SLOT_PARTS = 4
F32 = jnp.float32
BF16 = jnp.bfloat16


def dot_nn(a, b):
    return lax.dot_general(a, b, (((1,), (0,)), ((), ())), preferred_element_type=F32)


def dot_nt(a, b):
    return lax.dot_general(a, b, (((1,), (1,)), ((), ())), preferred_element_type=F32)


def two_parts(x):
    high = x.astype(BF16)
    low = (x - high.astype(F32)).astype(BF16)
    return jnp.concatenate([high, low], axis=0)


def spaced(lhs):
    zero = jnp.zeros_like(lhs[0])
    sides = [[x, zero] if n % 2 == 0 else [zero, x] for n, x in enumerate(lhs)]
    return jnp.concatenate([jnp.concatenate(x, axis=1) for x in sides], axis=0)


def square(a, b, c, d):
    return jnp.concatenate(
        [jnp.concatenate([a, b], axis=1), jnp.concatenate([c, d], axis=1)], axis=0
    )


def apart(out):
    rows, width = out.shape[0] // 4, out.shape[1] // 2
    return [out[n * rows : (n + 1) * rows, (n // 2) * width :][:, :width] for n in range(4)]


def four_nn(lhs, rhs):
    return apart(dot_nn(spaced(lhs), square(rhs[0], rhs[2], rhs[1], rhs[3])))


def four_nt(lhs, rhs):
    return apart(dot_nt(spaced(lhs), square(rhs[0], rhs[1], rhs[2], rhs[3])))


def kernel(
    groups,
    reps,
    factors_ref,
    virtuals_ref,
    occ_ref,
    energies_ref,
    orbitals_ref,
    ranks_ref,
    weight_ref,
    slots_ref,
    couplings_ref,
    rotations_hbm,
    margins_hbm,
    amp_hbm,
    dens_ref,
    rot,
    margin,
    turn,
    halves,
    sbuf,
    slots,
    local,
    integ,
    scale,
    afin,
    grams,
    dsend1,
    drecv1,
    dsend2,
    drecv2,
    dfin,
    load_sem,
    lay_sem,
    s1,
    r1,
    ys,
    yr,
    ss,
    sr,
    fs,
    fr,
    d1s,
    d1r,
    d2s,
    d2r,
    d3s,
    d3r,
):
    me = lax.axis_index("pairs")
    rep = lax.axis_index("rep")
    sides = 2 if reps % 2 == 0 else 1
    lanes = reps // sides
    side = lax.rem(rep, sides)
    lane = rep // sides
    orbs, aux = factors_ref.shape[:2]
    pairs, _, rank, _ = rot.shape
    coups = margin.shape[1]
    rows = rank // reps
    capa = slots_ref.shape[0]
    norb = groups * orbs
    share = pairs // reps
    row0 = pl.multiple_of(rep * rows, rows)

    def lane_rep(step):
        return lax.rem(lane + step + lanes, lanes) * sides + side

    twin = lane * sides + (1 - side)

    def send(src, dst, ssem, rsem, group, to_rep):
        return pltpu.make_async_remote_copy(
            src_ref=src,
            dst_ref=dst,
            send_sem=ssem,
            recv_sem=rsem,
            device_id=(group, to_rep),
            device_id_type=pl.DeviceIdType.MESH,
        )

    rot_copy = pltpu.make_async_copy(rotations_hbm, rot, load_sem.at[0])
    rot_copy.start()
    margin_copy = pltpu.make_async_copy(margins_hbm, margin, load_sem.at[1])
    margin_copy.start()

    barrier = pltpu.get_barrier_semaphore()

    def greet(k, carry):
        pl.semaphore_signal(
            barrier,
            inc=1,
            device_id=(lax.rem(me + k, groups), rep),
            device_id_type=pl.DeviceIdType.MESH,
        )
        return carry

    lax.fori_loop(1, groups, greet, 0)
    for j in range(1, reps):
        pl.semaphore_signal(
            barrier,
            inc=1,
            device_id=(me, lax.rem(rep + j, reps)),
            device_id_type=pl.DeviceIdType.MESH,
        )

    for o in range(orbs):
        half = dot_nn(factors_ref[o], virtuals_ref[o]).astype(BF16)
        level = jnp.broadcast_to(occ_ref[o : o + 1].astype(F32), (OCC_ROWS, rank))
        halves[0][o, :aux, :] = half
        halves[0][o, aux:, :] = level.astype(BF16)

    pl.semaphore_wait(barrier, groups - 1 + reps - 1)

    def group_copy(e, k, src, here):
        to = lax.rem(me + k, groups)
        return send(src(to), here(0, 0, k, 1), s1.at[e, k], r1.at[e, k], to, rep)

    def nearness(index, width):
        within = lax.rem(index, width)
        return lax.rem(width * (me + groups) - (index - within), width * groups) + within

    def spread(e, src, here, land, parts, between, ready):
        parts = parts if groups % parts == 0 else 1
        size = groups // parts

        def lane_copy(j, n):
            k = n * size
            return send(
                here(0, 0, k, size),
                land(j, 0, k, size),
                ys.at[e, j, n],
                yr.at[e, j, n],
                me,
                lane_rep(j),
            )

        def twin_copy(j, n):
            k = n * size
            return send(
                here(j, 0, k, size), land(j, 1, k, size), ss.at[e, j, n], sr.at[e, j, n], me, twin
            )

        def took(place, ssem, rsem):
            send(place, place, ssem, rsem, me, twin).wait_recv()

        def arrive(k, carry):
            between(k)
            took(here(0, 0, k, 1), s1.at[e, k], r1.at[e, k])
            return carry

        for n in range(parts):
            lax.fori_loop(max(n * size, 1), (n + 1) * size, arrive, 0)
            for j in range(1, lanes):
                lane_copy(j, n).start()
            if sides == 2:
                twin_copy(0, n).start()
        ready(0, 0)

        for j in range(1, lanes):
            for n in range(parts):
                took(here(j, 0, n * size, size), ys.at[e, j, n], yr.at[e, j, n])
                if sides == 2:
                    twin_copy(j, n).start()
            ready(j, 0)

        if sides == 2:
            for j in range(lanes):
                for n in range(parts):
                    took(here(j, 1, n * size, size), ss.at[e, j, n], sr.at[e, j, n])
                ready(j, 1)

        def sent_group(k, carry):
            group_copy(e, k, src, here).wait_send()
            return carry

        def finish():
            for n in range(parts):
                for j in range(1, lanes):
                    lane_copy(j, n).wait_send()
                if sides == 2:
                    for j in range(lanes):
                        twin_copy(j, n).wait_send()
            lax.fori_loop(1, groups, sent_group, 0)

        return finish

    def half_place(j, t, k, n):
        return halves[j * sides + t].at[pl.ds(k * orbs, n * orbs)]

    def half_source(d):
        return half_place(0, 0, 0, 1)

    def start_half(k, carry):
        group_copy(0, k, half_source, half_place).start()
        return carry

    lax.fori_loop(1, groups, start_half, 0)
    rot_copy.wait()
    flips = -(-pairs // max(groups - 1, 1))

    def flip(k):
        for step in range(flips):
            p = jnp.minimum((k - 1) * flips + step, pairs - 1)
            turn[p] = rot[p, 0].astype(F32).T.astype(BF16)

    row_at = lax.broadcasted_iota(jnp.int32, (rows, rank), 0) + row0
    column_at = lax.broadcasted_iota(jnp.int32, (rows, rank), 1)

    def integrate(j, t):
        block = halves[j * sides + t]
        last = j == lanes - 1 and t == sides - 1

        def step(n, carry):
            four = [4 * n + m for m in range(4)]
            left = [block[nearness(orbitals_ref[0, p], orbs)] for p in four]
            right = [block[nearness(orbitals_ref[1, p], orbs)] for p in four]
            turned = four_nt(
                [turn[p, pl.ds(row0, rows), :] for p in four], [x[:aux] for x in left]
            )
            mixed = four_nn([two_parts(x) for x in turned], [x[:aux] for x in right])
            mixed = [x[:rows] + x[rows:] for x in mixed]
            if j or t:
                mixed = [x + integ[p] for x, p in zip(mixed, four)]
            if not last:
                for x, p in zip(mixed, four):
                    integ[p] = x
                return carry
            values = four_nn([two_parts(x) for x in mixed], [rot[p, 1] for p in four])
            for m, p in enumerate(four):
                value = values[m][:rows] + values[m][rows:]
                occ = left[m][aux:].astype(F32)[:1] + right[m][aux:].astype(F32)[:1]
                first = energies_ref[p][:1]
                second = energies_ref[p][1:]
                first = jnp.sum(jnp.where(row_at == column_at, first, 0.0), axis=1, keepdims=True)
                live = (row_at < ranks_ref[0, p]) & (column_at < ranks_ref[0, p])
                factor = jnp.where(live, -1.0 / (first + second - occ), 0.0)
                integ[p] = value
                scale[p] = factor
                local[p] = (value * factor).astype(BF16)
            return carry

        lax.fori_loop(0, pairs // 4, step, 0, unroll=2)

    finish = spread(0, half_source, half_place, half_place, HALF_PARTS, flip, integrate)
    margin_copy.wait()

    def relax(it, p):
        items = [(p + n, c) for n in range(2) for c in range(coups)]
        lefts = []
        for at in range(0, len(items), 4):
            four = items[at : at + 4]
            got = four_nn(
                [margin[n, c, pl.ds(row0, rows), :] for n, c in four],
                [
                    slots[it][:, nearness(couplings_ref[c, n], capa)].reshape(rank, rank)
                    for n, c in four
                ],
            )
            lefts += [(weight_ref[c, n] * x).astype(BF16) for (n, c), x in zip(four, got)]
        two = [jnp.concatenate(lefts[n * coups : (n + 1) * coups], axis=1) for n in range(2)]
        wide = [
            jnp.concatenate([margin[p + n, c] for c in range(coups)], axis=1) for n in range(2)
        ]
        coupled = dot_nt(jnp.concatenate(two, axis=0), jnp.concatenate(wide, axis=0))
        parts = (coupled[:rows, :rank], coupled[rows:, rank:])
        return [
            ((integ[p + n] - parts[n]) * scale[p + n]).astype(BF16) for n in range(2)
        ]

    def deliver(it, earlier):
        e = (it + 1) % 2

        def slot_place(j, t, k, n):
            index = lax.rem(lane - j + lanes, lanes) * sides + (side if t == 0 else 1 - side)
            return slots[it].at[index, pl.ds(k * capa, n * capa)]

        def slot_land(j, t, k, n):
            return slot_place(0 if t == 0 else j, 0, k, n)

        def slot_source(d):
            return sbuf.at[it, d]

        def post(k, carry):
            to = lax.rem(me + k, groups)
            for s in range(capa):
                sbuf[it, to, s] = local[slots_ref[s, to]]
            group_copy(e, k, slot_source, slot_place).start()
            return carry

        lax.fori_loop(1, groups, post, 0)
        for s in range(capa):
            slots[it][rep, s] = local[slots_ref[s, me]]
        return spread(
            e,
            slot_source,
            slot_place,
            slot_land,
            SLOT_PARTS,
            lambda k: None,
            lambda j, t: earlier() if j == 0 and t == 0 else None,
        )

    for it in range(ITERS - 1):
        finish = deliver(it, finish)

        def step(n, carry, it=it):
            local[2 * n], local[2 * n + 1] = relax(it, 2 * n)
            return carry

        lax.fori_loop(0, pairs // 2, step, 0, unroll=UNROLL // 2)

    finish = deliver(ITERS - 1, finish)

    def piece(r, chunk):
        return afin.at[r, pl.ds(chunk * share, share)]

    def final_lane(j, chunk):
        block = piece(rep, chunk)
        return send(block, block, fs.at[j, chunk], fr.at[j, chunk], me, lane_rep(j))

    def final_twin(j, chunk):
        block = piece(lane_rep(-j), chunk)
        index = lanes + j
        return send(block, block, fs.at[index, chunk], fr.at[index, chunk], me, twin)

    def relay_final(chunk):
        for j in range(1, lanes):
            block = piece(lane_rep(-j), chunk)
            send(block, block, fs.at[j, chunk], fr.at[j, chunk], me, twin).wait_recv()
            if sides == 2:
                final_twin(j, chunk).start()

    def settle_final(chunk):
        if sides == 2:
            for j in range(lanes):
                other = lax.rem(lane - j + lanes, lanes) * sides + (1 - side)
                block = piece(other, chunk)
                index = lanes + j
                send(block, block, fs.at[index, chunk], fr.at[index, chunk], me, twin).wait_recv()

    def last_chunk(step, carry):
        turn_lane = lax.rem(lane + 1 + step // sides, lanes)
        turn_side = lax.rem(side + step, sides)
        chunk = turn_lane * sides + turn_side
        base = chunk * share
        for k in range(0, share, 2):
            afin[rep, base + k], afin[rep, base + k + 1] = relax(ITERS - 1, base + k)
        for j in range(1, lanes):
            final_lane(j, chunk).start()
        if sides == 2:
            final_twin(0, chunk).start()
        return carry

    lax.fori_loop(0, reps, last_chunk, 0)
    if sides == 2:
        relay_final(twin)
    relay_final(rep)
    settle_final(rep)
    base = rep * share

    def gram(n, carry):
        four = [4 * n + m for m in range(4)]
        amps = [afin[:, base + k].reshape(rank, rank) for k in four]
        left = four_nn([rot[base + k, 0] for k in four], amps)
        right = four_nt([rot[base + k, 1] for k in four], amps)
        for s, sides_of in enumerate((left, right)):
            rounded = [x.astype(BF16) for x in sides_of]
            for k, x in zip(four, four_nt(rounded, rounded)):
                grams[2 * k + s] = x * (1.0 / rank)
        return carry

    lax.fori_loop(0, share // 4, gram, 0, unroll=2)

    def collect(o, carry):
        for r in range(reps):
            span = slice(r * rows, (r + 1) * rows)
            total = jnp.zeros((rows, rank), F32)
            for k in range(share):
                for s in range(2):
                    named = orbitals_ref[s, base + k] == o
                    total = total + jnp.where(named, grams[2 * k + s, span, :], 0.0)
            dsend1[r, o] = total.astype(BF16)
        return carry

    lax.fori_loop(0, norb, collect, 0)

    def density_rep(j):
        to = lax.rem(rep + j, reps)
        return send(dsend1.at[to], drecv1.at[rep], d1s.at[j], d1r.at[j], me, to)

    for j in range(1, reps):
        density_rep(j).start()
    drecv1[rep] = dsend1[rep]

    def rest(step, carry):
        relay_final(lax.rem(lane + step, lanes) * sides + side)
        if sides == 2:
            relay_final(lax.rem(lane + step, lanes) * sides + 1 - side)
        return carry

    lax.fori_loop(1, lanes, rest, 0)
    for j in range(1, reps):
        block = drecv1.at[lax.rem(rep - j + reps, reps)]
        send(block, block, d1s.at[j], d1r.at[j], me, rep).wait_recv()

    def density_group(k):
        to = lax.rem(me + k, groups)
        return send(dsend2.at[to], drecv2.at[me], d2s.at[k], d2r.at[k], to, rep)

    def rep_sum(d):
        total = jnp.zeros((orbs, rows, rank), F32)
        for r in range(reps):
            total = total + drecv1[r, pl.ds(d * orbs, orbs)].astype(F32)
        return total

    def post_density(k, carry):
        to = lax.rem(me + k, groups)
        dsend2[to] = rep_sum(to).astype(BF16)
        density_group(k).start()
        return carry

    lax.fori_loop(1, groups, post_density, 0)
    own = rep_sum(me)

    def take_density(k, total):
        q = lax.rem(me - k + groups, groups)
        block = drecv2.at[q]
        send(block, block, d2s.at[k], d2r.at[k], me, rep).wait_recv()
        return total + drecv2[q].astype(F32)

    dfin[rep] = lax.fori_loop(1, groups, take_density, own)

    def settle_rest(step, carry):
        settle_final(lax.rem(rep + step, reps))
        return carry

    def lay(r):
        return pltpu.make_async_copy(
            afin.at[r], amp_hbm.at[:, pl.ds(r * rows, rows), :], lay_sem.at[r]
        )

    def density_last(j):
        to = lax.rem(rep + j, reps)
        return send(dfin.at[rep], dfin.at[rep], d3s.at[j], d3r.at[j], me, to)

    for j in range(1, reps):
        density_last(j).start()
    lax.fori_loop(1, reps, settle_rest, 0)
    for r in range(reps):
        lay(r).start()
    for j in range(1, reps):
        block = dfin.at[lax.rem(rep - j + reps, reps)]
        send(block, block, d3s.at[j], d3r.at[j], me, rep).wait_recv()
    for r in range(reps):
        dens_ref[:, r * rows : (r + 1) * rows, :] = dfin[r]

    finish()
    for r in range(reps):
        lay(r).wait()
    for chunk in range(reps):
        for j in range(1, lanes):
            final_lane(j, chunk).wait_send()
        if sides == 2:
            for j in range(lanes):
                final_twin(j, chunk).wait_send()
    for j in range(1, reps):
        density_rep(j).wait_send()
        density_last(j).wait_send()

    def sent_density(k, carry):
        density_group(k).wait_send()
        return carry

    lax.fori_loop(1, groups, sent_density, 0)


def hand_over(reps, amp_in, dens_in, amp_out, dens_out, sem):
    part = amp_in.shape[0] // reps
    copies = [
        pltpu.make_async_copy(
            amp_in.at[pl.ds(r * part, part)], amp_out.at[pl.ds(r * part, part)], sem.at[r]
        )
        for r in range(reps)
    ]
    copies.append(pltpu.make_async_copy(dens_in, dens_out, sem.at[reps]))
    for copy in copies:
        copy.start()
    for copy in copies:
        copy.wait()


def body(
    factors,
    orbital_virtuals,
    occupied,
    pair_rotations,
    pair_energies,
    pair_orbitals,
    pair_ranks,
    margins,
    coupling_weight,
    send_slots,
    couplings,
):
    groups = lax.axis_size("pairs")
    reps = lax.axis_size("rep")
    orbs, aux, _ = factors.shape
    pairs, _, rank, _ = pair_rotations.shape
    coups = margins.shape[1]
    capa = send_slots.shape[2]
    rows = rank // reps
    norb = groups * orbs
    share = pairs // reps
    sides = 2 if reps % 2 == 0 else 1
    lanes = reps // sides
    vmem = pl.BlockSpec(memory_space=pltpu.VMEM)
    smem = pl.BlockSpec(memory_space=pltpu.SMEM)
    anywhere = pl.BlockSpec(memory_space=pl.ANY)
    dma = pltpu.SemaphoreType.DMA
    results = pl.pallas_call(
        functools.partial(kernel, groups, reps),
        out_shape=(
            jax.ShapeDtypeStruct((pairs, rank, rank), BF16),
            jax.ShapeDtypeStruct((orbs, rank, rank), F32),
        ),
        in_specs=[vmem] * 4 + [smem] * 5 + [anywhere] * 2,
        out_specs=(anywhere, vmem),
        scratch_shapes=[
            pltpu.VMEM(pair_rotations.shape, BF16),
            pltpu.VMEM(margins.shape, BF16),
            pltpu.VMEM((pairs, rank, rank), BF16),
            tuple(pltpu.VMEM((norb, aux + OCC_ROWS, rank), BF16) for _ in range(reps)),
            pltpu.VMEM((ITERS, groups, capa, rows, rank), BF16),
            tuple(
                pltpu.VMEM((reps, groups * capa, rows, rank), BF16) for _ in range(ITERS)
            ),
            pltpu.VMEM((pairs, rows, rank), BF16),
            pltpu.VMEM((pairs, rows, rank), F32),
            pltpu.VMEM((pairs, rows, rank), F32),
            pltpu.VMEM((reps, pairs, rows, rank), BF16),
            pltpu.VMEM((2 * share, rank, rank), F32),
            pltpu.VMEM((reps, norb, rows, rank), BF16),
            pltpu.VMEM((reps, norb, rows, rank), BF16),
            pltpu.VMEM((groups, orbs, rows, rank), BF16),
            pltpu.VMEM((groups, orbs, rows, rank), BF16),
            pltpu.VMEM((reps, orbs, rows, rank), F32),
            dma((2,)),
            dma((reps,)),
            dma((2, groups)),
            dma((2, groups)),
            dma((2, lanes, max(HALF_PARTS, SLOT_PARTS))),
            dma((2, lanes, max(HALF_PARTS, SLOT_PARTS))),
            dma((2, lanes, max(HALF_PARTS, SLOT_PARTS))),
            dma((2, lanes, max(HALF_PARTS, SLOT_PARTS))),
            dma((2 * lanes, reps)),
            dma((2 * lanes, reps)),
            dma((reps,)),
            dma((reps,)),
            dma((groups,)),
            dma((groups,)),
            dma((reps,)),
            dma((reps,)),
        ],
        compiler_params=pltpu.CompilerParams(
            collective_id=0, has_side_effects=True, vmem_limit_bytes=60 * 1024 * 1024
        ),
        cost_estimate=pl.CostEstimate(
            flops=4 * pairs * coups * ITERS * rows * rank * rank,
            bytes_accessed=2 * pairs * coups * rank * rank,
            transcendentals=0,
        ),
    )(
        factors,
        orbital_virtuals,
        occupied[:, None],
        pair_energies,
        pair_orbitals.T,
        pair_ranks[None, :],
        coupling_weight.T,
        send_slots[0].T,
        couplings.T,
        pair_rotations,
        margins,
    )
    return pl.pallas_call(
        functools.partial(hand_over, reps),
        out_shape=tuple(jax.ShapeDtypeStruct(x.shape, x.dtype) for x in results),
        in_specs=[anywhere] * 2,
        out_specs=(anywhere, anywhere),
        scratch_shapes=[dma((reps + 1,))],
        compiler_params=pltpu.CompilerParams(vmem_limit_bytes=60 * 1024 * 1024),
    )(*results)


def solution(mesh):
    return jax.shard_map(
        body,
        mesh=mesh,
        in_specs=(
            P("pairs", "rep", None),
            P("pairs", None, None),
            P("pairs"),
            P("pairs", None, None, None),
            P("pairs", None, None),
            P("pairs", None),
            P("pairs"),
            P("pairs", None, None, None),
            P("pairs", None),
            P("pairs", None, None),
            P("pairs", None),
        ),
        out_specs=(P("pairs", None, None), P("pairs", None, None)),
        check_vma=False,
    )
```

```python
import functools

import jax
import jax.numpy as jnp
from jax import lax
from jax.experimental import pallas as pl
from jax.experimental.pallas import tpu as pltpu
from jax.sharding import PartitionSpec as P

ITERS = 3
OCC_ROWS = 16
UNROLL = 8
HALF_PARTS = 8
SLOT_PARTS = 4
F32 = jnp.float32
BF16 = jnp.bfloat16


def dot_nn(a, b):
    return lax.dot_general(a, b, (((1,), (0,)), ((), ())), preferred_element_type=F32)


def dot_nt(a, b):
    return lax.dot_general(a, b, (((1,), (1,)), ((), ())), preferred_element_type=F32)


def two_parts(x):
    high = x.astype(BF16)
    low = (x - high.astype(F32)).astype(BF16)
    return jnp.concatenate([high, low], axis=0)


def spaced(lhs):
    zero = jnp.zeros_like(lhs[0])
    sides = [[x, zero] if n % 2 == 0 else [zero, x] for n, x in enumerate(lhs)]
    return jnp.concatenate([jnp.concatenate(x, axis=1) for x in sides], axis=0)


def square(a, b, c, d):
    return jnp.concatenate(
        [jnp.concatenate([a, b], axis=1), jnp.concatenate([c, d], axis=1)], axis=0
    )


def apart(out):
    rows, width = out.shape[0] // 4, out.shape[1] // 2
    return [out[n * rows : (n + 1) * rows, (n // 2) * width :][:, :width] for n in range(4)]


def four_nn(lhs, rhs):
    return apart(dot_nn(spaced(lhs), square(rhs[0], rhs[2], rhs[1], rhs[3])))


def four_nt(lhs, rhs):
    return apart(dot_nt(spaced(lhs), square(rhs[0], rhs[1], rhs[2], rhs[3])))


def kernel(
    groups,
    reps,
    factors_ref,
    virtuals_ref,
    occ_ref,
    energies_ref,
    orbitals_ref,
    ranks_ref,
    weight_ref,
    slots_ref,
    couplings_ref,
    rotations_hbm,
    margins_hbm,
    amp_hbm,
    dens_ref,
    rot,
    margin,
    turn,
    halves,
    sbuf,
    slots,
    local,
    integ,
    scale,
    afin,
    grams,
    dsend1,
    drecv1,
    dsend2,
    drecv2,
    dfin,
    load_sem,
    lay_sem,
    s1,
    r1,
    ys,
    yr,
    ss,
    sr,
    fs,
    fr,
    d1s,
    d1r,
    d2s,
    d2r,
    d3s,
    d3r,
):
    me = lax.axis_index("pairs")
    rep = lax.axis_index("rep")
    sides = 2 if reps % 2 == 0 else 1
    lanes = reps // sides
    side = lax.rem(rep, sides)
    lane = rep // sides
    orbs, aux = factors_ref.shape[:2]
    pairs, _, rank, _ = rot.shape
    coups = margin.shape[1]
    rows = rank // reps
    capa = slots_ref.shape[0]
    norb = groups * orbs
    share = pairs // reps
    row0 = pl.multiple_of(rep * rows, rows)

    def lane_rep(step):
        return lax.rem(lane + step + lanes, lanes) * sides + side

    twin = lane * sides + (1 - side)

    def send(src, dst, ssem, rsem, group, to_rep):
        return pltpu.make_async_remote_copy(
            src_ref=src,
            dst_ref=dst,
            send_sem=ssem,
            recv_sem=rsem,
            device_id=(group, to_rep),
            device_id_type=pl.DeviceIdType.MESH,
        )

    rot_copy = pltpu.make_async_copy(rotations_hbm, rot, load_sem.at[0])
    rot_copy.start()
    margin_copy = pltpu.make_async_copy(margins_hbm, margin, load_sem.at[1])
    margin_copy.start()

    barrier = pltpu.get_barrier_semaphore()

    def greet(k, carry):
        pl.semaphore_signal(
            barrier,
            inc=1,
            device_id=(lax.rem(me + k, groups), rep),
            device_id_type=pl.DeviceIdType.MESH,
        )
        return carry

    lax.fori_loop(1, groups, greet, 0)
    for j in range(1, reps):
        pl.semaphore_signal(
            barrier,
            inc=1,
            device_id=(me, lax.rem(rep + j, reps)),
            device_id_type=pl.DeviceIdType.MESH,
        )

    for o in range(orbs):
        half = dot_nn(factors_ref[o], virtuals_ref[o]).astype(BF16)
        level = jnp.broadcast_to(occ_ref[o : o + 1].astype(F32), (OCC_ROWS, rank))
        halves[0][o, :aux, :] = half
        halves[0][o, aux:, :] = level.astype(BF16)

    pl.semaphore_wait(barrier, groups - 1 + reps - 1)

    def group_copy(e, k, src, here):
        to = lax.rem(me + k, groups)
        return send(src(to), here(0, 0, k, 1), s1.at[e, k], r1.at[e, k], to, rep)

    def nearness(index, width):
        within = lax.rem(index, width)
        return lax.rem(width * (me + groups) - (index - within), width * groups) + within

    def spread(e, src, here, land, parts, between, ready):
        parts = parts if groups % parts == 0 else 1
        size = groups // parts

        def lane_copy(j, n):
            k = n * size
            return send(
                here(0, 0, k, size),
                land(j, 0, k, size),
                ys.at[e, j, n],
                yr.at[e, j, n],
                me,
                lane_rep(j),
            )

        def twin_copy(j, n):
            k = n * size
            return send(
                here(j, 0, k, size), land(j, 1, k, size), ss.at[e, j, n], sr.at[e, j, n], me, twin
            )

        def took(place, ssem, rsem):
            send(place, place, ssem, rsem, me, twin).wait_recv()

        def arrive(k, carry):
            between(k)
            took(here(0, 0, k, 1), s1.at[e, k], r1.at[e, k])
            return carry

        for n in range(parts):
            lax.fori_loop(max(n * size, 1), (n + 1) * size, arrive, 0)
            for j in range(1, lanes):
                lane_copy(j, n).start()
            if sides == 2:
                twin_copy(0, n).start()
        ready(0, 0)

        for j in range(1, lanes):
            for n in range(parts):
                took(here(j, 0, n * size, size), ys.at[e, j, n], yr.at[e, j, n])
                if sides == 2:
                    twin_copy(j, n).start()
            ready(j, 0)

        if sides == 2:
            for j in range(lanes):
                for n in range(parts):
                    took(here(j, 1, n * size, size), ss.at[e, j, n], sr.at[e, j, n])
                ready(j, 1)

        def sent_group(k, carry):
            group_copy(e, k, src, here).wait_send()
            return carry

        def finish():
            for n in range(parts):
                for j in range(1, lanes):
                    lane_copy(j, n).wait_send()
                if sides == 2:
                    for j in range(lanes):
                        twin_copy(j, n).wait_send()
            lax.fori_loop(1, groups, sent_group, 0)

        return finish

    def half_place(j, t, k, n):
        return halves[j * sides + t].at[pl.ds(k * orbs, n * orbs)]

    def half_source(d):
        return half_place(0, 0, 0, 1)

    def start_half(k, carry):
        group_copy(0, k, half_source, half_place).start()
        return carry

    lax.fori_loop(1, groups, start_half, 0)
    rot_copy.wait()
    flips = -(-pairs // max(groups - 1, 1))

    def flip(k):
        for step in range(flips):
            p = jnp.minimum((k - 1) * flips + step, pairs - 1)
            turn[p] = rot[p, 0].astype(F32).T.astype(BF16)

    row_at = lax.broadcasted_iota(jnp.int32, (rows, rank), 0) + row0
    column_at = lax.broadcasted_iota(jnp.int32, (rows, rank), 1)

    def integrate(j, t):
        block = halves[j * sides + t]
        last = j == lanes - 1 and t == sides - 1

        def step(n, carry):
            four = [4 * n + m for m in range(4)]
            left = [block[nearness(orbitals_ref[0, p], orbs)] for p in four]
            right = [block[nearness(orbitals_ref[1, p], orbs)] for p in four]
            turned = four_nt(
                [turn[p, pl.ds(row0, rows), :] for p in four], [x[:aux] for x in left]
            )
            mixed = four_nn([two_parts(x) for x in turned], [x[:aux] for x in right])
            mixed = [x[:rows] + x[rows:] for x in mixed]
            if j or t:
                mixed = [x + integ[p] for x, p in zip(mixed, four)]
            if not last:
                for x, p in zip(mixed, four):
                    integ[p] = x
                return carry
            values = four_nn([two_parts(x) for x in mixed], [rot[p, 1] for p in four])
            for m, p in enumerate(four):
                value = values[m][:rows] + values[m][rows:]
                occ = left[m][aux:].astype(F32)[:1] + right[m][aux:].astype(F32)[:1]
                first = energies_ref[p][:1]
                second = energies_ref[p][1:]
                first = jnp.sum(jnp.where(row_at == column_at, first, 0.0), axis=1, keepdims=True)
                live = (row_at < ranks_ref[0, p]) & (column_at < ranks_ref[0, p])
                factor = jnp.where(live, -1.0 / (first + second - occ), 0.0)
                integ[p] = value
                scale[p] = factor
                local[p] = (value * factor).astype(BF16)
            return carry

        lax.fori_loop(0, pairs // 4, step, 0, unroll=2)

    finish = spread(0, half_source, half_place, half_place, HALF_PARTS, flip, integrate)
    margin_copy.wait()

    def relax(it, p):
        items = [(p + n, c) for n in range(2) for c in range(coups)]
        lefts = []
        for at in range(0, len(items), 4):
            four = items[at : at + 4]
            got = four_nn(
                [margin[n, c, pl.ds(row0, rows), :] for n, c in four],
                [
                    slots[it][:, nearness(couplings_ref[c, n], capa)].reshape(rank, rank)
                    for n, c in four
                ],
            )
            lefts += [(weight_ref[c, n] * x).astype(BF16) for (n, c), x in zip(four, got)]
        two = [jnp.concatenate(lefts[n * coups : (n + 1) * coups], axis=1) for n in range(2)]
        wide = [
            jnp.concatenate([margin[p + n, c] for c in range(coups)], axis=1) for n in range(2)
        ]
        coupled = dot_nt(jnp.concatenate(two, axis=0), jnp.concatenate(wide, axis=0))
        parts = (coupled[:rows, :rank], coupled[rows:, rank:])
        return [
            ((integ[p + n] - parts[n]) * scale[p + n]).astype(BF16) for n in range(2)
        ]

    def deliver(it, earlier):
        e = (it + 1) % 2

        def slot_place(j, t, k, n):
            index = lax.rem(lane - j + lanes, lanes) * sides + (side if t == 0 else 1 - side)
            return slots[it].at[index, pl.ds(k * capa, n * capa)]

        def slot_land(j, t, k, n):
            return slot_place(0 if t == 0 else j, 0, k, n)

        def slot_source(d):
            return sbuf.at[it, d]

        def post(k, carry):
            to = lax.rem(me + k, groups)
            for s in range(capa):
                sbuf[it, to, s] = local[slots_ref[s, to]]
            group_copy(e, k, slot_source, slot_place).start()
            return carry

        lax.fori_loop(1, groups, post, 0)
        for s in range(capa):
            slots[it][rep, s] = local[slots_ref[s, me]]
        return spread(
            e,
            slot_source,
            slot_place,
            slot_land,
            SLOT_PARTS,
            lambda k: None,
            lambda j, t: earlier() if j == 0 and t == 0 else None,
        )

    for it in range(ITERS - 1):
        finish = deliver(it, finish)

        def step(n, carry, it=it):
            local[2 * n], local[2 * n + 1] = relax(it, 2 * n)
            return carry

        lax.fori_loop(0, pairs // 2, step, 0, unroll=UNROLL // 2)

    finish = deliver(ITERS - 1, finish)

    def piece(r, chunk):
        return afin.at[r, pl.ds(chunk * share, share)]

    def final_lane(j, chunk):
        block = piece(rep, chunk)
        return send(block, block, fs.at[j, chunk], fr.at[j, chunk], me, lane_rep(j))

    def final_twin(j, chunk):
        block = piece(lane_rep(-j), chunk)
        index = lanes + j
        return send(block, block, fs.at[index, chunk], fr.at[index, chunk], me, twin)

    def relay_final(chunk):
        for j in range(1, lanes):
            block = piece(lane_rep(-j), chunk)
            send(block, block, fs.at[j, chunk], fr.at[j, chunk], me, twin).wait_recv()
            if sides == 2:
                final_twin(j, chunk).start()

    def settle_final(chunk):
        if sides == 2:
            for j in range(lanes):
                other = lax.rem(lane - j + lanes, lanes) * sides + (1 - side)
                block = piece(other, chunk)
                index = lanes + j
                send(block, block, fs.at[index, chunk], fr.at[index, chunk], me, twin).wait_recv()

    def last_chunk(step, carry):
        turn_lane = lax.rem(lane + 1 + step // sides, lanes)
        turn_side = lax.rem(side + step, sides)
        chunk = turn_lane * sides + turn_side
        base = chunk * share
        for k in range(0, share, 2):
            afin[rep, base + k], afin[rep, base + k + 1] = relax(ITERS - 1, base + k)
        for j in range(1, lanes):
            final_lane(j, chunk).start()
        if sides == 2:
            final_twin(0, chunk).start()
        return carry

    lax.fori_loop(0, reps, last_chunk, 0)
    if sides == 2:
        relay_final(twin)
    relay_final(rep)
    settle_final(rep)
    base = rep * share

    def gram(n, carry):
        four = [4 * n + m for m in range(4)]
        amps = [afin[:, base + k].reshape(rank, rank) for k in four]
        left = four_nn([rot[base + k, 0] for k in four], amps)
        right = four_nt([rot[base + k, 1] for k in four], amps)
        for s, sides_of in enumerate((left, right)):
            rounded = [x.astype(BF16) for x in sides_of]
            for k, x in zip(four, four_nt(rounded, rounded)):
                grams[2 * k + s] = x * (1.0 / rank)
        return carry

    lax.fori_loop(0, share // 4, gram, 0, unroll=2)

    def collect(o, carry):
        for r in range(reps):
            span = slice(r * rows, (r + 1) * rows)
            total = jnp.zeros((rows, rank), F32)
            for k in range(share):
                for s in range(2):
                    named = orbitals_ref[s, base + k] == o
                    total = total + jnp.where(named, grams[2 * k + s, span, :], 0.0)
            dsend1[r, o] = total.astype(BF16)
        return carry

    lax.fori_loop(0, norb, collect, 0)

    def density_rep(j):
        to = lax.rem(rep + j, reps)
        return send(dsend1.at[to], drecv1.at[rep], d1s.at[j], d1r.at[j], me, to)

    for j in range(1, reps):
        density_rep(j).start()
    drecv1[rep] = dsend1[rep]

    def rest(step, carry):
        relay_final(lax.rem(lane + step, lanes) * sides + side)
        if sides == 2:
            relay_final(lax.rem(lane + step, lanes) * sides + 1 - side)
        return carry

    lax.fori_loop(1, lanes, rest, 0)
    for j in range(1, reps):
        block = drecv1.at[lax.rem(rep - j + reps, reps)]
        send(block, block, d1s.at[j], d1r.at[j], me, rep).wait_recv()

    def density_group(k):
        to = lax.rem(me + k, groups)
        return send(dsend2.at[to], drecv2.at[me], d2s.at[k], d2r.at[k], to, rep)

    def rep_sum(d):
        total = jnp.zeros((orbs, rows, rank), F32)
        for r in range(reps):
            total = total + drecv1[r, pl.ds(d * orbs, orbs)].astype(F32)
        return total

    def post_density(k, carry):
        to = lax.rem(me + k, groups)
        dsend2[to] = rep_sum(to).astype(BF16)
        density_group(k).start()
        return carry

    lax.fori_loop(1, groups, post_density, 0)
    own = rep_sum(me)

    def take_density(k, total):
        q = lax.rem(me - k + groups, groups)
        block = drecv2.at[q]
        send(block, block, d2s.at[k], d2r.at[k], me, rep).wait_recv()
        return total + drecv2[q].astype(F32)

    dfin[rep] = lax.fori_loop(1, groups, take_density, own)

    def settle_rest(step, carry):
        settle_final(lax.rem(rep + step, reps))
        return carry

    def lay(r):
        return pltpu.make_async_copy(
            afin.at[r], amp_hbm.at[:, pl.ds(r * rows, rows), :], lay_sem.at[r]
        )

    def density_last(j):
        to = lax.rem(rep + j, reps)
        return send(dfin.at[rep], dfin.at[rep], d3s.at[j], d3r.at[j], me, to)

    for j in range(1, reps):
        density_last(j).start()
    lax.fori_loop(1, reps, settle_rest, 0)
    for r in range(reps):
        lay(r).start()
    for j in range(1, reps):
        block = dfin.at[lax.rem(rep - j + reps, reps)]
        send(block, block, d3s.at[j], d3r.at[j], me, rep).wait_recv()
    for r in range(reps):
        dens_ref[:, r * rows : (r + 1) * rows, :] = dfin[r]

    finish()
    for r in range(reps):
        lay(r).wait()
    for chunk in range(reps):
        for j in range(1, lanes):
            final_lane(j, chunk).wait_send()
        if sides == 2:
            for j in range(lanes):
                final_twin(j, chunk).wait_send()
    for j in range(1, reps):
        density_rep(j).wait_send()
        density_last(j).wait_send()

    def sent_density(k, carry):
        density_group(k).wait_send()
        return carry

    lax.fori_loop(1, groups, sent_density, 0)


def hand_over(amp_in, dens_in, amp_out, dens_out):
    amp_out[...] = amp_in[...]
    dens_out[...] = dens_in[...]


def body(
    factors,
    orbital_virtuals,
    occupied,
    pair_rotations,
    pair_energies,
    pair_orbitals,
    pair_ranks,
    margins,
    coupling_weight,
    send_slots,
    couplings,
):
    groups = lax.axis_size("pairs")
    reps = lax.axis_size("rep")
    orbs, aux, _ = factors.shape
    pairs, _, rank, _ = pair_rotations.shape
    coups = margins.shape[1]
    capa = send_slots.shape[2]
    rows = rank // reps
    norb = groups * orbs
    share = pairs // reps
    sides = 2 if reps % 2 == 0 else 1
    lanes = reps // sides
    vmem = pl.BlockSpec(memory_space=pltpu.VMEM)
    smem = pl.BlockSpec(memory_space=pltpu.SMEM)
    anywhere = pl.BlockSpec(memory_space=pl.ANY)
    dma = pltpu.SemaphoreType.DMA
    results = pl.pallas_call(
        functools.partial(kernel, groups, reps),
        out_shape=(
            jax.ShapeDtypeStruct((pairs, rank, rank), BF16),
            jax.ShapeDtypeStruct((orbs, rank, rank), F32),
        ),
        in_specs=[vmem] * 4 + [smem] * 5 + [anywhere] * 2,
        out_specs=(anywhere, vmem),
        scratch_shapes=[
            pltpu.VMEM(pair_rotations.shape, BF16),
            pltpu.VMEM(margins.shape, BF16),
            pltpu.VMEM((pairs, rank, rank), BF16),
            tuple(pltpu.VMEM((norb, aux + OCC_ROWS, rank), BF16) for _ in range(reps)),
            pltpu.VMEM((ITERS, groups, capa, rows, rank), BF16),
            tuple(
                pltpu.VMEM((reps, groups * capa, rows, rank), BF16) for _ in range(ITERS)
            ),
            pltpu.VMEM((pairs, rows, rank), BF16),
            pltpu.VMEM((pairs, rows, rank), F32),
            pltpu.VMEM((pairs, rows, rank), F32),
            pltpu.VMEM((reps, pairs, rows, rank), BF16),
            pltpu.VMEM((2 * share, rank, rank), F32),
            pltpu.VMEM((reps, norb, rows, rank), BF16),
            pltpu.VMEM((reps, norb, rows, rank), BF16),
            pltpu.VMEM((groups, orbs, rows, rank), BF16),
            pltpu.VMEM((groups, orbs, rows, rank), BF16),
            pltpu.VMEM((reps, orbs, rows, rank), F32),
            dma((2,)),
            dma((reps,)),
            dma((2, groups)),
            dma((2, groups)),
            dma((2, lanes, max(HALF_PARTS, SLOT_PARTS))),
            dma((2, lanes, max(HALF_PARTS, SLOT_PARTS))),
            dma((2, lanes, max(HALF_PARTS, SLOT_PARTS))),
            dma((2, lanes, max(HALF_PARTS, SLOT_PARTS))),
            dma((2 * lanes, reps)),
            dma((2 * lanes, reps)),
            dma((reps,)),
            dma((reps,)),
            dma((groups,)),
            dma((groups,)),
            dma((reps,)),
            dma((reps,)),
        ],
        compiler_params=pltpu.CompilerParams(
            collective_id=0, has_side_effects=True, vmem_limit_bytes=60 * 1024 * 1024
        ),
        cost_estimate=pl.CostEstimate(
            flops=4 * pairs * coups * ITERS * rows * rank * rank,
            bytes_accessed=2 * pairs * coups * rank * rank,
            transcendentals=0,
        ),
    )(
        factors,
        orbital_virtuals,
        occupied[:, None],
        pair_energies,
        pair_orbitals.T,
        pair_ranks[None, :],
        coupling_weight.T,
        send_slots[0].T,
        couplings.T,
        pair_rotations,
        margins,
    )
    return pl.pallas_call(
        hand_over,
        out_shape=tuple(jax.ShapeDtypeStruct(x.shape, x.dtype) for x in results),
        in_specs=[vmem] * 2,
        out_specs=(vmem, vmem),
        compiler_params=pltpu.CompilerParams(vmem_limit_bytes=60 * 1024 * 1024),
    )(*results)


def solution(mesh):
    return jax.shard_map(
        body,
        mesh=mesh,
        in_specs=(
            P("pairs", "rep", None),
            P("pairs", None, None),
            P("pairs"),
            P("pairs", None, None, None),
            P("pairs", None, None),
            P("pairs", None),
            P("pairs"),
            P("pairs", None, None, None),
            P("pairs", None),
            P("pairs", None, None),
            P("pairs", None),
        ),
        out_specs=(P("pairs", None, None), P("pairs", None, None)),
        check_vma=False,
    )
```
